128 devices in a mesh: hid: 4 (over y_lo, core), tok: 32 (over y_hi, x, z).
Axes of the slice: x: 4, y: 4 (y_hi: 2, y_lo: 2; y = y_hi * 2 + y_lo), z: 4, core: 2. Of those that a mesh axis runs over, the one named last changes fastest.
Arguments:
- activations: bfloat16 [32768, 14336], P('tok', 'hid'), may hold values from -6 to 6
- dictionary: bfloat16 [14336, 1024], P('hid', 'tok'), may hold values from -0.046875 to 0.046875
- second_factor: bfloat16 [1024, 256], replicated, may hold values from -0.1875 to 0.1875
- first_codes: float32 [32, 4, 256, 1024], P('tok', 'hid'), may hold values from 0.05 to 2
- second_codes: float32 [32, 4, 256, 256], P('tok', 'hid'), may hold values from 0.05 to 2
Outputs:
- first_new: float32 [32, 4, 256, 1024], P('tok', 'hid')
- second_new: float32 [32, 4, 256, 256], P('tok', 'hid')
- direction: float32 [1024, 256], P('tok')
The draws below stay inside these ranges and needn't reach their ends.
All inputs are finite; a program needn't handle non-finite values.
Results may differ from the reference program's by a relative error of at most 0.00057.
Values may be sent and summed in bfloat16 or wider, within the bound.
A program may use at most 128 MiB of HBM per device.

```python
import math
import jax
import jax.numpy as jnp
from jax import lax

D = 14336
K1 = 1024
K2 = 256
TOK_DEV = 1024
TOKENS = 32768
SUB = 256
N_HID = 4
N_TOK = 32


def levels(key, extent, pieces, smallest, top_value):
    level, own = 1.0, jax.random.fold_in(key, 6)
    for dim, shards_of in pieces:
        heights = jnp.exp(jax.random.uniform(jax.random.fold_in(own, dim), (shards_of,), jnp.float32, smallest / len(pieces), top_value / len(pieces)))
        level = level * jnp.repeat(heights, extent[dim] // shards_of).reshape([-1 if axis == dim else 1 for axis in range(len(extent))])
    return level


def normal_values(rng, dims, spread, reach, cuts=(), held_as=jnp.bfloat16):
    drawn = jax.random.normal(rng, dims, jnp.float32) * spread
    if len(cuts) > 0:
        drawn = levels(rng, dims, cuts, -0.22, 0.18) * drawn
    return jnp.clip(drawn, min=-reach, max=reach).astype(held_as)


def setup_inputs(seed: int = 0) -> dict:
    seeds = jax.random.split(jax.random.key(seed), 6)
    activations = normal_values(seeds[0], (TOKENS, D), 1.0, 6.0, ((0, 32), (1, 4)))
    dictionary = normal_values(seeds[1], (D, K1), D ** -0.5, 0.046875, ((0, 4), (1, 32)))
    second_factor = normal_values(seeds[2], (K1, K2), K1 ** -0.5, 0.1875)
    first_codes = jnp.clip(jnp.exp(math.log(2.0) - 3.6888794 * jax.random.uniform(seeds[3], (N_TOK, N_HID, SUB, K1), jnp.float32) ** levels(seeds[3], (N_TOK, N_HID, SUB, K1), ((0, 32), (1, 4)), -0.2, 0.2)), 0.05, 2.0)
    second_codes = jnp.clip(jnp.exp(math.log(2.0) - 3.6888794 * jax.random.uniform(seeds[4], (N_TOK, N_HID, SUB, K2), jnp.float32) ** levels(seeds[4], (N_TOK, N_HID, SUB, K2), ((0, 32), (1, 4)), -0.2, 0.2)), 0.05, 2.0)
    return dict(activations=activations, dictionary=dictionary, second_factor=second_factor, first_codes=first_codes, second_codes=second_codes)


HIGH = lax.Precision.HIGHEST

def mult_update(codes, lin, gmat):
    num = jnp.maximum(lin, 0.0) + jnp.dot(codes, jnp.maximum(-gmat, 0.0), precision=HIGH)
    den = jnp.maximum(-lin, 0.0) + jnp.dot(codes, jnp.maximum(gmat, 0.0), precision=HIGH)
    return codes * jnp.sqrt(num / den)

def reference(activations, dictionary, second_factor, first_codes, second_codes):
    blocks = activations.reshape(TOKENS // TOK_DEV, TOK_DEV, D)
    feats = lax.map(lambda blk: jnp.dot(blk, dictionary, preferred_element_type=jnp.float32).astype(jnp.bfloat16), blocks).reshape(TOKENS, K1)
    gram = jnp.dot(dictionary.T, dictionary, preferred_element_type=jnp.float32)
    ffull = feats.astype(jnp.float32)
    first_flat = first_codes.reshape(TOKENS, K1)
    first_new = mult_update(first_flat, ffull, gram)
    proj = jnp.dot(feats, second_factor, preferred_element_type=jnp.float32)
    sfull = second_factor.astype(jnp.float32)
    inner = jnp.dot(jnp.dot(sfull.T, gram, precision=HIGH), sfull, precision=HIGH)
    second_flat = second_codes.reshape(TOKENS, K2)
    second_new = mult_update(second_flat, proj, inner)
    cross = jnp.dot(ffull.T, second_new, precision=HIGH)
    codegram = jnp.dot(second_new.T, second_new, precision=HIGH)
    grad = jnp.dot(jnp.dot(gram, sfull, precision=HIGH), codegram, precision=HIGH) - cross
    direction = grad / jnp.sqrt(jnp.mean(grad * grad) + 1e-06)
    return (first_new.reshape(first_codes.shape), second_new.reshape(second_codes.shape), direction)
```

```python
import functools

import jax
import jax.numpy as jnp
from jax import lax
from jax.experimental import pallas as pl
from jax.experimental.pallas import tpu as pltpu
from jax.sharding import PartitionSpec as P

F32 = jnp.float32
BF16 = jnp.bfloat16
MESH = pl.DeviceIdType.MESH
NN = (((1,), (0,)), ((), ()))
NT = (((1,), (1,)), ((), ()))


def dot(a, b, dims=NN):
    return lax.dot_general(a, b, dims, preferred_element_type=F32)


def split(a):
    hi = a.astype(BF16)
    return hi, (a - hi.astype(F32)).astype(BF16)


def dot3(a, b, dims=NN):
    ah, al = a
    bh, bl = b
    return dot(ah, bh, dims) + (dot(al, bh, dims) + dot(ah, bl, dims))


def pos_neg(g):
    p = split(jnp.maximum(g, 0.0))
    n = split(jnp.maximum(-g, 0.0))
    return p, n


def kernel(
    act_hbm, dt_hbm, s_hbm, h1_hbm, h2_hbm,
    first_hbm, second_hbm, dir_hbm,
    act, w, s, h1, h2,
    pl_f, pl_g, rc_f, rc_g, ys_f, ys_g, ry_f, ry_g,
    fp, gown, sp, st, perm, eye, h1h, h1l, fn, ft,
    gsb, gb, first_v, second_v,
    gp, rcgp, gs1, r1a, r1b, ab2, r2a, r2b, ab3, r3, dirh, dirf,
    nrm, nrx, nrz, nry, nrc,
    local_sem, ga_send, ga_recv, fe_send, fe_recv, gs_send, gs_recv, gg_send, gg_recv,
    rs_send, rs_recv, no_send, no_recv,
):
    hid = lax.axis_index("hid")
    tok = lax.axis_index("tok")
    yl, c = hid // 2, hid % 2
    yh, x, z = tok // 16, (tok // 4) % 4, tok % 4
    y = yh * 2 + yl
    sub = h1.shape[0]

    def dev(yl_, c_, yh_, x_, z_):
        return (yl_ * 2 + c_, yh_ * 16 + x_ * 4 + z_)

    core = dev(yl, 1 - c, yh, x, z)
    ylp = dev(1 - yl, c, yh, x, z)
    yhp = dev(yl, c, 1 - yh, x, z)

    def xdev(d):
        return dev(yl, c, yh, (x + d) % 4, z)

    def zdev(d):
        return dev(yl, c, yh, x, (z + d) % 4)

    def ydev(d):
        yy = (y + d) % 4
        return dev(yy % 2, c, yy // 2, x, z)

    acopy = pltpu.make_async_copy(act_hbm, act, local_sem.at[0])
    acopy.start()
    own_b = yh * 16 + x * 4 + z
    dcopy = pltpu.make_async_copy(dt_hbm, w.at[own_b], local_sem.at[1])
    dcopy.start()
    scopy = pltpu.make_async_copy(s_hbm, s, local_sem.at[2])
    scopy.start()
    h1copy = pltpu.make_async_copy(h1_hbm, h1, local_sem.at[3])
    h1copy.start()
    h2copy = pltpu.make_async_copy(h2_hbm, h2, local_sem.at[4])
    h2copy.start()

    barrier = pltpu.get_barrier_semaphore()
    for d in (1, 2, 3):
        for who in (xdev(d), zdev(d), ydev(d)):
            pl.semaphore_signal(barrier, inc=1, device_id=who, device_id_type=MESH)
    pl.semaphore_signal(barrier, inc=1, device_id=core, device_id_type=MESH)
    pl.semaphore_wait(barrier, 10)

    pending = []

    def send(src, dst, ss, rs, who):
        cp = pltpu.make_async_remote_copy(
            src_ref=src, dst_ref=dst, send_sem=ss, recv_sem=rs, device_id=who, device_id_type=MESH
        )
        cp.start()
        pending.append(cp)
        return cp

    def part(o):
        p = (yh + o) % 2
        u = x + p * (z - x)
        v = z + p * (x - z)
        return p, u, v

    def blk(p, u_, v_):
        return p * 16 + u_ * (4 - 3 * p) + v_ * (1 + 3 * p)

    DU = (0, 3, 1, 2)

    def gdev(o, du, dv):
        p, u, v = part(o)
        u_, v_ = (u + du) % 4, (v + dv) % 4
        return (hid, yh * 16 + u_ * (4 - 3 * p) + v_ * (1 + 3 * p))

    def gsend(o, k, b, who, rows=None, src=None):
        dst = w.at[b] if rows is None else w.at[b, pl.ds(rows, 16)]
        if src is None:
            src = dst
        return send(src, dst, ga_send.at[o, k], ga_recv.at[o, k], who)

    def gblk(o, du, dv):
        p, u, v = part(o)
        return blk(p, (u + du) % 4, (v + dv) % 4)

    gd = {}

    def start_ph1(o, src=None):
        b = gblk(o, 0, 0)
        gd[o, 0] = gsend(o, 0, b, gdev(o, 1, 0), src=src)
        gd[o, 1] = gsend(o, 1, b, gdev(o, 3, 0), src=src)

    def start_ph2(o, i, src=None):
        b = gblk(o, DU[i], 0)
        gd[o, 4 + 4 * i] = gsend(o, 4 + 4 * i, b, gdev(o, 0, 1), src=src)
        gd[o, 5 + 4 * i] = gsend(o, 5 + 4 * i, b, gdev(o, 0, 3), src=src)

    def fwd_ph1(o):
        gd[o, 0].wait_recv()
        gd[o, 2] = gsend(o, 2, gblk(o, 3, 0), gdev(o, 1, 0), rows=0)
        gd[o, 1].wait_recv()
        gd[o, 3] = gsend(o, 3, gblk(o, 1, 0), gdev(o, 3, 0), rows=16)

    def fwd_ph2(o, i):
        gd[o, 4 + 4 * i].wait_recv()
        gd[o, 6 + 4 * i] = gsend(o, 6 + 4 * i, gblk(o, DU[i], 3), gdev(o, 0, 1), rows=0)
        gd[o, 5 + 4 * i].wait_recv()
        gd[o, 7 + 4 * i] = gsend(o, 7 + 4 * i, gblk(o, DU[i], 1), gdev(o, 0, 3), rows=16)

    def end_ph1(o):
        gd[o, 2].wait_recv()
        gd[o, 3].wait_recv()

    def end_ph2(o, i):
        gd[o, 6 + 4 * i].wait_recv()
        gd[o, 7 + 4 * i].wait_recv()

    fd = {}

    def chunk_of(o, i):
        p, u, v = part(o)
        return p * 4 + (u + DU[i]) % 4

    def group(i):
        def rows_of(o):
            return jnp.concatenate([w[gblk_abs(o, i, j)] for j in range(4)], axis=0)

        def gblk_abs(o, i, j):
            p, u, v = part(o)
            return blk(p, (u + DU[i]) % 4, j)

        def weights():
            return jnp.concatenate([rows_of(0), rows_of(1)], axis=0)

        lrows = jnp.concatenate([w[x * 4 + z], w[16 + x * 4 + z]], axis=0)
        g = dot(lrows, weights(), NT)
        pl_g[i] = g.reshape(2, 32, g.shape[1])
        fd[i, 0] = send(pl_g.at[i, 1 - c], rc_g.at[i], fe_send.at[i, 0], fe_recv.at[i, 0], core)

        def body(h, carry):
            pl_f[i, h // 2, h % 2] = dot(act[pl.ds(pl.multiple_of(h * sub, sub), sub), :], weights(), NT)
            return carry

        lax.fori_loop(0, 4, body, 0)
        fd[i, 1] = send(pl_f.at[i, :, 1 - c], rc_f.at[i], fe_send.at[i, 1], fe_recv.at[i, 1], core)

    def reduce_core_g(i):
        fd[i, 0].wait_recv()
        ys_g[i] = pl_g[i, c] + rc_g[i]
        fd[i, 2] = send(ys_g.at[i], ry_g.at[i], fe_send.at[i, 2], fe_recv.at[i, 2], ylp)

    def reduce_core_f(i):
        fd[i, 1].wait_recv()
        ys_f[i] = pl_f[i, 1 - yl, c] + rc_f[i, 1 - yl]
        fd[i, 3] = send(ys_f.at[i], ry_f.at[i], fe_send.at[i, 3], fe_recv.at[i, 3], ylp)

    def lanes(q):
        return pl.ds(pl.multiple_of(q * 128, 128), 128)

    def reduce_y_g(i):
        fd[i, 2].wait_recv()
        g = ys_g[i] + ry_g[i]
        gown[:, lanes(chunk_of(0, i))] = g[:, :128]
        gown[:, lanes(chunk_of(1, i))] = g[:, 128:]

    def reduce_y_f(i):
        fd[i, 3].wait_recv()
        f = ((pl_f[i, yl, c] + rc_f[i, yl]) + ry_f[i]).astype(BF16)
        fp[:, lanes(chunk_of(0, i))] = f[:, :128]
        fp[:, lanes(chunk_of(1, i))] = f[:, 128:]

    start_ph1(0, src=dt_hbm)
    yh_copy = send(dt_hbm, w.at[own_b], ga_send.at[0, 20], ga_recv.at[0, 20], yhp)
    start_ph2(0, 0, src=dt_hbm)

    scopy.wait()
    h1copy.wait()
    n_i = lax.broadcasted_iota(jnp.int32, (512, 512), 0)
    r_i = lax.broadcasted_iota(jnp.int32, (512, 512), 1)
    swapped = ((n_i // 32) % 4) * 128 + (n_i // 128) * 32 + n_i % 32
    perm[...] = (r_i == swapped).astype(F32).astype(BF16)
    eye[...] = (r_i == n_i).astype(F32).astype(BF16)
    yh_copy.wait_recv()
    start_ph1(1)
    start_ph2(1, 0)
    dcopy.wait()
    sp[0:512] = s[0:512]
    for a in range(4):
        for b in range(4):
            sp[512 + a * 128 + b * 32:512 + a * 128 + b * 32 + 32] = s[512 + b * 128 + a * 32:512 + b * 128 + a * 32 + 32]
    hh, hl = split(h1[...])
    h1h[:, :512] = hh[:, :512]
    h1l[:, :512] = hl[:, :512]
    h1h[:, 512:] = dot(hh[:, 512:], perm[...]).astype(BF16)
    h1l[:, 512:] = dot(hl[:, 512:], perm[...]).astype(BF16)

    fwd_ph1(0)
    fwd_ph2(0, 0)
    fwd_ph1(1)
    fwd_ph2(1, 0)
    for i in (1, 2):
        start_ph2(0, i)
        start_ph2(1, i)
    end_ph1(0)
    end_ph1(1)
    end_ph2(0, 0)
    end_ph2(1, 0)
    acopy.wait()
    group(0)
    start_ph2(0, 3)
    start_ph2(1, 3)
    fwd_ph2(0, 1)
    fwd_ph2(1, 1)
    reduce_core_g(0)
    reduce_core_f(0)
    st[...] = s[...].astype(F32).T.astype(BF16)
    end_ph2(0, 1)
    end_ph2(1, 1)
    group(1)
    fwd_ph2(0, 2)
    fwd_ph2(1, 2)
    reduce_y_g(0)
    reduce_y_f(0)
    reduce_core_g(1)
    reduce_core_f(1)
    end_ph2(0, 2)
    end_ph2(1, 2)
    group(2)
    fwd_ph2(0, 3)
    fwd_ph2(1, 3)
    reduce_y_g(1)
    reduce_y_f(1)
    reduce_core_g(2)
    reduce_core_f(2)
    end_ph2(0, 3)
    end_ph2(1, 3)
    group(3)
    reduce_core_g(3)
    reduce_y_g(2)
    reduce_y_g(3)

    def dot2(a, b):
        ah, al = split(a)
        return dot(ah, b) + dot(al, b)

    gsb[c, x, z] = dot2(gown[...], sp[...])
    gb[c, x, z] = gown[...]

    def gather_ph1(buf, half, ss, rs):
        cps = []
        for d in (1, 3, 2):
            a = buf.at[c, x, z, :, pl.ds(0, half)]
            b = buf.at[c, x, z, :, pl.ds(half, half)]
            cps.append(send(a, a, ss.at[d - 1], rs.at[d - 1], xdev(d)))
            cps.append(send(b, b, ss.at[3 + d - 1], rs.at[3 + d - 1], zdev(d)))
        return cps

    def gather_ph2(buf, half, ss, rs):
        cps = []
        for d in (1, 3, 2):
            a = buf.at[c, :, z, :, pl.ds(0, half)]
            b = buf.at[c, x, :, :, pl.ds(half, half)]
            cps.append(send(a, a, ss.at[6 + d - 1], rs.at[6 + d - 1], zdev(d)))
            cps.append(send(b, b, ss.at[9 + d - 1], rs.at[9 + d - 1], xdev(d)))
        return cps

    def gather_core(buf, ss, rs):
        return send(buf.at[c], buf.at[c], ss.at[12], rs.at[12], core)

    def wait_all(cps):
        for cp in cps:
            cp.wait_recv()

    g1 = gather_ph1(gsb, 128, gs_send, gs_recv)
    reduce_core_f(3)
    h2copy.wait()
    reduce_y_f(2)
    wait_all(g1)
    g2 = gather_ph2(gsb, 128, gs_send, gs_recv)
    gg1 = gather_ph1(gb, 512, gg_send, gg_recv)
    reduce_y_f(3)
    fn[:, :512] = fp[:, :512]
    fn[:, 512:] = dot(fp[:, 512:], perm[...]).astype(BF16)
    ft[:512] = dot(eye[...], fp[:, :512], NT).astype(BF16)
    ft[512:] = dot(perm[...], fp[:, 512:], NT).astype(BF16)
    proj = dot(fp[...], sp[...])
    wait_all(g2)
    g3 = gather_core(gsb, gs_send, gs_recv)
    wait_all(gg1)
    gg2 = gather_ph2(gb, 512, gg_send, gg_recv)
    g3.wait_recv()

    width = h2.shape[1]
    gs = gsb[...].reshape(1024, width)
    gsh, gsl = split(gs)
    inner = dot(st[...], gsh) + dot(st[...], gsl)
    ip, im = pos_neg(inner)
    h2v = h2[...]
    h2s = split(h2v)
    num = jnp.maximum(proj, 0.0) + dot3(h2s, im)
    den = jnp.maximum(-proj, 0.0) + dot3(h2s, ip)
    second_v[...] = h2v * jnp.sqrt(num / den)
    second_copy = pltpu.make_async_copy(second_v, second_hbm, local_sem.at[5])
    second_copy.start()

    def grad_body(j, carry):
        sn = split(second_v[...])
        rows = gsb[j // 2, pl.ds((j % 2) * 2, 2)].reshape(256, width)
        res = dot3(split(rows), sn, NT) - ft[pl.ds(pl.multiple_of(j * 256, 256), 256), :].astype(F32)
        g = dot3(split(res), sn)
        gp[0, j // 2, pl.ds((j % 2) * 2, 2)] = g[:, :128].reshape(2, 4, 32, 128)
        gp[1, j // 2, pl.ds((j % 2) * 2, 2)] = g[:, 128:].reshape(2, 4, 32, 128)
        return carry

    lax.fori_loop(0, 4, grad_body, 0)
    k1 = send(gp.at[1 - c], rcgp, rs_send.at[0], rs_recv.at[0], core)
    wait_all(gg2)
    gg3 = gather_core(gb, gg_send, gg_recv)
    k1.wait_recv()
    gs1[...] = gp[c] + rcgp[...]
    k2 = []
    for d in (1, 3, 2):
        k2.append(send(gs1.at[0, (x + d) % 4], r1a.at[d - 1], rs_send.at[d], rs_recv.at[d], xdev(d)))
        k2.append(send(gs1.at[1, :, (z + d) % 4], r1b.at[d - 1], rs_send.at[3 + d], rs_recv.at[3 + d], zdev(d)))
    gg3.wait_recv()

    def first_chunk(j):
        rows = gb[j // 2, pl.ds((j % 2) * 2, 2)].reshape(256, 1024)
        gpos, gneg = pos_neg(rows)
        hs = (h1h[...], h1l[...])
        cols = pl.ds(pl.multiple_of(j * 256, 256), 256)
        f = fn[:, cols].astype(F32)
        num_ = jnp.maximum(f, 0.0) + dot3(hs, gneg, NT)
        den_ = jnp.maximum(-f, 0.0) + dot3(hs, gpos, NT)
        first_v[:, cols] = h1[:, cols] * jnp.sqrt(num_ / den_)

    wait_all(k2)
    ab2[0] = (gs1[0, x] + r1a[0]) + (r1a[1] + r1a[2])
    ab2[1] = (gs1[1, :, z] + r1b[0]) + (r1b[1] + r1b[2])
    k3 = []
    for d in (1, 3, 2):
        k3.append(send(ab2.at[0, (z + d) % 4], r2a.at[d - 1], rs_send.at[6 + d], rs_recv.at[6 + d], zdev(d)))
        k3.append(send(ab2.at[1, (x + d) % 4], r2b.at[d - 1], rs_send.at[9 + d], rs_recv.at[9 + d], xdev(d)))
    wait_all(k3)
    ab3[0] = (ab2[0, z] + r2a[0]) + (r2a[1] + r2a[2])
    ab3[1] = (ab2[1, x] + r2b[0]) + (r2b[1] + r2b[2])
    k4 = []
    for d in (1, 3, 2):
        k4.append(send(ab3.at[((y + d) % 4) // 2], r3.at[d - 1], rs_send.at[12 + d], rs_recv.at[12 + d], ydev(d)))
    wait_all(k4)
    own = (ab3[yh] + r3[0]) + (r3[1] + r3[2])
    dirh[c] = own
    k5 = send(dirh.at[c], dirh.at[c], rs_send.at[16], rs_recv.at[16], core)

    sq = own * own
    nrm[0] = (sq[0:8] + sq[8:16]) + (sq[16:24] + sq[24:32])
    n1 = [send(nrm.at[0], nrx.at[d - 1], no_send.at[d - 1], no_recv.at[d - 1], xdev(d)) for d in (1, 3, 2)]
    wait_all(n1)
    nrm[1] = (nrm[0] + nrx[0]) + (nrx[1] + nrx[2])
    n2 = [send(nrm.at[1], nrz.at[d - 1], no_send.at[2 + d], no_recv.at[2 + d], zdev(d)) for d in (1, 3, 2)]
    wait_all(n2)
    nrm[2] = (nrm[1] + nrz[0]) + (nrz[1] + nrz[2])
    n3 = send(nrm.at[2], nry, no_send.at[6], no_recv.at[6], yhp)
    n3.wait_recv()
    nrm[3] = nrm[2] + nry[...]
    n4 = send(nrm.at[3], nrc, no_send.at[7], no_recv.at[7], core)
    n4.wait_recv()
    total = jnp.sum(nrm[3] + nrc[...])
    scale = jnp.sqrt(total / (1024 * width) + 1e-06)
    k5.wait_recv()
    dirf[:, :128] = dirh[0] / scale
    dirf[:, 128:] = dirh[1] / scale
    dir_copy = pltpu.make_async_copy(dirf, dir_hbm, local_sem.at[6])
    dir_copy.start()

    def first_body(j, carry):
        first_chunk(j)
        return carry

    lax.fori_loop(0, 4, first_body, 0)
    first_copy = pltpu.make_async_copy(first_v, first_hbm, local_sem.at[7])
    first_copy.start()
    for cp in pending:
        cp.wait_send()
    second_copy.wait()
    dir_copy.wait()
    first_copy.wait()


def shards(activations, dictionary, second_factor, first_codes, second_codes):
    tokens, rows = activations.shape
    sub, k1 = first_codes.shape[2:]
    k2 = second_codes.shape[3]
    v, dma = pltpu.VMEM, pltpu.SemaphoreType.DMA
    scratch = [
        v((tokens, rows), BF16), v((32, 32, rows), BF16), v((k1, k2), BF16), v((sub, k1), F32), v((sub, k2), F32),
        v((4, 2, 2, sub, 256), F32), v((4, 2, 32, 256), F32),
        v((4, 2, sub, 256), F32), v((4, 32, 256), F32),
        v((4, sub, 256), F32), v((4, 32, 256), F32),
        v((4, sub, 256), F32), v((4, 32, 256), F32),
        v((sub, k1), BF16), v((32, k1), F32), v((k1, k2), BF16), v((k2, k1), BF16),
        v((512, 512), BF16), v((512, 512), BF16), v((sub, k1), BF16), v((sub, k1), BF16),
        v((sub, k1), BF16), v((k1, sub), BF16),
        v((2, 4, 4, 32, k2), F32), v((2, 4, 4, 32, k1), F32), v((sub, k1), F32), v((sub, k2), F32),
        v((2, 2, 4, 4, 32, 128), F32), v((2, 4, 4, 32, 128), F32), v((2, 4, 4, 32, 128), F32),
        v((3, 4, 32, 128), F32), v((3, 4, 32, 128), F32), v((2, 4, 32, 128), F32),
        v((3, 32, 128), F32), v((3, 32, 128), F32), v((2, 32, 128), F32), v((3, 32, 128), F32),
        v((2, 32, 128), F32), v((32, 256), F32),
        v((4, 8, 128), F32), v((3, 8, 128), F32), v((3, 8, 128), F32), v((8, 128), F32), v((8, 128), F32),
        dma((8,)), dma((2, 21)), dma((2, 21)), dma((4, 4)), dma((4, 4)), dma((13,)), dma((13,)), dma((13,)), dma((13,)),
        dma((17,)), dma((17,)), dma((8,)), dma((8,)),
    ]
    hbm = pl.BlockSpec(memory_space=pl.ANY)
    first, second, direction = pl.pallas_call(
        kernel,
        out_shape=(
            jax.ShapeDtypeStruct((sub, k1), F32),
            jax.ShapeDtypeStruct((sub, k2), F32),
            jax.ShapeDtypeStruct((32, k2), F32),
        ),
        in_specs=[hbm] * 5,
        out_specs=(hbm,) * 3,
        scratch_shapes=scratch,
        compiler_params=pltpu.CompilerParams(
            collective_id=0, has_side_effects=True, vmem_limit_bytes=60 * 1024 * 1024
        ),
        name="sweep",
    )(activations, dictionary.T, second_factor, first_codes.reshape(sub, k1), second_codes.reshape(sub, k2))
    return first.reshape(first_codes.shape), second.reshape(second_codes.shape), direction


def solution(mesh):
    in_specs = (
        P("tok", "hid"),
        P("hid", "tok"),
        P(),
        P("tok", "hid", None, None),
        P("tok", "hid", None, None),
    )
    out_specs = (P("tok", "hid", None, None), P("tok", "hid", None, None), P("tok", None))
    return jax.shard_map(shards, mesh=mesh, in_specs=in_specs, out_specs=out_specs, check_vma=False)
```

```python
import functools

import jax
import jax.numpy as jnp
from jax import lax
from jax.experimental import pallas as pl
from jax.experimental.pallas import tpu as pltpu
from jax.sharding import PartitionSpec as P

F32 = jnp.float32
BF16 = jnp.bfloat16
MESH = pl.DeviceIdType.MESH
NN = (((1,), (0,)), ((), ()))
NT = (((1,), (1,)), ((), ()))


def dot(a, b, dims=NN):
    return lax.dot_general(a, b, dims, preferred_element_type=F32)


def split(a):
    hi = a.astype(BF16)
    return hi, (a - hi.astype(F32)).astype(BF16)


def dot3(a, b, dims=NN):
    ah, al = a
    bh, bl = b
    return dot(ah, bh, dims) + (dot(al, bh, dims) + dot(ah, bl, dims))


def pos_neg(g):
    p = split(jnp.maximum(g, 0.0))
    n = split(jnp.maximum(-g, 0.0))
    return p, n


ORDER = (
    (2, 1), (0, 2, 0, 1, 1), (0, 2, 0, 0, 1), (0, 1, 0, 1), (0, 1, 1, 1), (0, 2, 0, 1, 0), (0, 1, 0, 0),
    (0, 2, 0, 0, 0), (2, 0), (0, 1, 1, 0), (4, 0), (4, 1), (1, 1, 0, 1), (1, 1, 1, 1), (1, 2, 0, 0, 1), (0, 1, 2, 1),
    (1, 2, 0, 1, 1), (1, 1, 0, 0), (1, 1, 1, 0), (0, 2, 2, 1, 1), (1, 2, 0, 0, 0), (0, 1, 2, 0), (0, 2, 1, 0, 0),
    (0, 2, 1, 1, 1), (0, 2, 0, 2, 1), (0, 2, 0, 2, 0), (1, 2, 1, 1, 1), (1, 1, 2, 1), (1, 2, 0, 1, 0),
    (0, 2, 1, 0, 1), (1, 2, 1, 0, 0), (1, 2, 0, 2, 0), (1, 2, 0, 2, 1), (1, 2, 2, 0, 0), (1, 2, 1, 0, 1),
    (1, 2, 2, 1, 1), (0, 2, 2, 0, 0), (0, 2, 1, 1, 0), (4, 2), (1, 2, 1, 2, 1), (1, 2, 1, 2, 0), (0, 2, 1, 2, 0),
    (3, 0, 0), (1, 1, 2, 0), (1, 2, 1, 1, 0), (0, 2, 1, 2, 1), (0, 2, 2, 0, 1), (1, 2, 2, 0, 1), (3, 0, 1),
    (1, 2, 2, 2, 1), (0, 2, 2, 1, 0), (0, 2, 2, 2, 0), (1, 2, 2, 2, 0), (1, 2, 2, 1, 0), (0, 2, 2, 2, 1),
    (0, 2, 3, 1, 1), (3, 0, 2), (0, 2, 3, 0, 0), (3, 0, 3), (0, 2, 3, 0, 1), (3, 1, 0), (0, 2, 3, 1, 0),
    (1, 2, 3, 0, 0), (1, 2, 3, 1, 1), (1, 2, 3, 1, 0), (1, 2, 3, 0, 1), (3, 1, 1), (3, 1, 2), (3, 1, 3), (3, 2, 0),
    (0, 2, 3, 2, 1), (0, 2, 3, 2, 0), (1, 2, 3, 2, 0), (1, 2, 3, 2, 1), (3, 2, 1), (3, 2, 2), (3, 2, 3), (3, 3, 0),
    (3, 3, 1), (3, 3, 2), (3, 3, 3),
)


def kernel(
    act_hbm, dt_hbm, s_hbm, h1_hbm, h2_hbm,
    first_hbm, second_hbm, dir_hbm,
    act, w, s, h1, h2,
    pl_f, pl_g, rc_f, rc_g, ys_f, ry_f,
    fp, gown, sp, st, perm, eye, h1h, h1l, fn, ft,
    gsb, gb, dg, first_v, second_v,
    gp, rcgp, gs1, r1a, r1b, ab2, r2a, r2b, ab3, r3, fin, dirh, dirf,
    nrm, nrr, nrc,
    local_sem, ga_send, ga_recv, fe_send, fe_recv, gs_send, gs_recv, gg_send, gg_recv,
    dg_send, dg_recv, rs_send, rs_recv, no_send, no_recv,
):
    hid = lax.axis_index("hid")
    tok = lax.axis_index("tok")
    yl, c = hid // 2, hid % 2
    yh, x, z = tok // 16, (tok // 4) % 4, tok % 4
    y = yh * 2 + yl
    sub = h1.shape[0]
    width = h2.shape[1]

    def dev(yl_, c_, yh_, x_, z_):
        return (yl_ * 2 + c_, yh_ * 16 + x_ * 4 + z_)

    core = dev(yl, 1 - c, yh, x, z)
    ylp = dev(1 - yl, c, yh, x, z)
    ylc = dev(1 - yl, 1 - c, yh, x, z)
    yhp = dev(yl, c, 1 - yh, x, z)

    def plane(dx, dz):
        return dev(yl, c, yh, (x + dx) % 4, (z + dz) % 4)

    def xdev(d):
        return plane(d, 0)

    def zdev(d):
        return plane(0, d)

    def ydev(d):
        yy = (y + d) % 4
        return dev(yy % 2, c, yy // 2, x, z)

    own_b = yh * 16 + x * 4 + z
    dcopy = pltpu.make_async_copy(dt_hbm, w.at[own_b], local_sem.at[1])
    dcopy.start()
    scopy = pltpu.make_async_copy(s_hbm, s, local_sem.at[2])
    scopy.start()
    h1copy = pltpu.make_async_copy(h1_hbm, h1, local_sem.at[3])
    h1copy.start()
    h2copy = pltpu.make_async_copy(h2_hbm, h2, local_sem.at[4])
    h2copy.start()
    acopy = pltpu.make_async_copy(act_hbm, act, local_sem.at[0])
    acopy.start()

    barrier = pltpu.get_barrier_semaphore()
    peers = [plane(dx, dz) for dx in range(4) for dz in range(4) if dx + dz > 0]
    peers += [ydev(1), ydev(2), ydev(3), core, ylc]
    for who in peers:
        pl.semaphore_signal(barrier, inc=1, device_id=who, device_id_type=MESH)
    pl.semaphore_wait(barrier, len(peers))

    pending = []

    def send(src, dst, ss, rs, who):
        cp = pltpu.make_async_remote_copy(
            src_ref=src, dst_ref=dst, send_sem=ss, recv_sem=rs, device_id=who, device_id_type=MESH
        )
        cp.start()
        pending.append(cp)
        return cp

    def settle():
        for cp in pending:
            cp.wait_send()
        pending.clear()

    def wait_all(cps):
        for cp in cps:
            cp.wait_recv()

    def part(o):
        p = (yh + o) % 2
        u = x + p * (z - x)
        v = z + p * (x - z)
        return p, u, v

    def blk(p, u_, v_):
        return p * 16 + u_ * (4 - 3 * p) + v_ * (1 + 3 * p)

    DU = (0, 3, 1, 2)

    def gdev(o, du, dv):
        p, u, v = part(o)
        u_, v_ = (u + du) % 4, (v + dv) % 4
        return (hid, yh * 16 + u_ * (4 - 3 * p) + v_ * (1 + 3 * p))

    def gblk(o, du, dv):
        p, u, v = part(o)
        return blk(p, (u + du) % 4, (v + dv) % 4)

    gd = {}
    arrived = set()

    def need(*key):
        if key not in arrived:
            arrived.add(key)
            gd[key].wait_recv()

    def gsend(key, k, b, who, r, hbm=False):
        o = key[0]
        dst = w.at[b, pl.ds(16 * r, 16)]
        src = dt_hbm.at[pl.ds(16 * r, 16)] if hbm else dst
        gd[key] = send(src, dst, ga_send.at[o, k], ga_recv.at[o, k], who)

    def own_here(o, r):
        if o == 1:
            need(2, r)

    def step(key):
        o = key[0]
        if o == 2:
            gsend(key, key[1], own_b, yhp, key[1], True)
        elif key[1] == 1:
            _, _, sg, r = key
            if sg < 2:
                own_here(o, r)
                gsend(key, sg * 2 + r, gblk(o, 0, 0), gdev(o, 3 if sg else 1, 0), r, o == 0)
            else:
                need(o, 1, r, r)
                gsend(key, 4 + r, gblk(o, 1 if r else 3, 0), gdev(o, 3 if r else 1, 0), r)
        else:
            _, _, i, sg, r = key
            k = 6 + 6 * i
            if sg < 2:
                if i == 0:
                    own_here(o, r)
                elif i < 3:
                    need(o, 1, i - 1, r)
                else:
                    need(o, 1, 2, r)
                gsend(key, k + sg * 2 + r, gblk(o, DU[i], 0), gdev(o, 0, 3 if sg else 1), r, o == 0 and i == 0)
            else:
                need(o, 2, i, r, r)
                gsend(key, k + 4 + r, gblk(o, DU[i], 1 if r else 3), gdev(o, 0, 3 if r else 1), r)

    def need_group(i):
        for o in (0, 1):
            for r in (0, 1):
                own_here(o, r)
                if i in (1, 2):
                    need(o, 1, i - 1, r)
                if i == 3:
                    need(o, 1, 2, r)
                for sg in (0, 1, 2):
                    need(o, 2, i, sg, r)

    fd = {}

    def chunk_of(o, i):
        p, u, v = part(o)
        return p * 4 + (u + DU[i]) % 4

    def weights(i):
        rows = []
        for o in (0, 1):
            p, u, v = part(o)
            rows += [w[blk(p, (u + DU[i]) % 4, j)] for j in range(4)]
        return jnp.concatenate(rows, axis=0)

    def group_g(i):
        need_group(i)
        lrows = jnp.concatenate([w[x * 4 + z], w[16 + x * 4 + z]], axis=0)
        g = dot(lrows, weights(i), NT)
        pl_g[i] = g.reshape(2, 32, g.shape[1])
        fd[i, 0] = send(pl_g.at[i, 1 - c], rc_g.at[i, 0], fe_send.at[i, 0], fe_recv.at[i, 0], core)
        fd[i, 1] = send(pl_g.at[i, c], rc_g.at[i, 1], fe_send.at[i, 1], fe_recv.at[i, 1], ylp)
        fd[i, 2] = send(pl_g.at[i, 1 - c], rc_g.at[i, 2], fe_send.at[i, 2], fe_recv.at[i, 2], ylc)

    def group_f(i, other):
        cc = 1 - c if other else c
        a = act[:, cc].reshape(2 * sub, act.shape[3])
        pl_f[i, cc] = dot(a, weights(i), NT).reshape(2, sub, 256)
        if other:
            fd[i, 3] = send(pl_f.at[i, cc], rc_f.at[i], fe_send.at[i, 3], fe_recv.at[i, 3], core)

    def reduce_core(i):
        fd[i, 3].wait_recv()
        ys_f[i] = pl_f[i, c, 1 - yl] + rc_f[i, 1 - yl]
        fd[i, 4] = send(ys_f.at[i], ry_f.at[i], fe_send.at[i, 4], fe_recv.at[i, 4], ylp)

    def lanes(q):
        return pl.ds(pl.multiple_of(q * 128, 128), 128)

    def reduce_g(i):
        for k in range(3):
            fd[i, k].wait_recv()
        g = (pl_g[i, c] + rc_g[i, 0]) + (rc_g[i, 1] + rc_g[i, 2])
        gown[:, lanes(chunk_of(0, i))] = g[:, :128]
        gown[:, lanes(chunk_of(1, i))] = g[:, 128:]

    def reduce_f(i):
        fd[i, 4].wait_recv()
        f = ((pl_f[i, c, yl] + rc_f[i, yl]) + ry_f[i]).astype(BF16)
        fp[:, lanes(chunk_of(0, i))] = f[:, :128]
        fp[:, lanes(chunk_of(1, i))] = f[:, 128:]

    def prepare_a():
        n_i = lax.broadcasted_iota(jnp.int32, (512, 512), 0)
        r_i = lax.broadcasted_iota(jnp.int32, (512, 512), 1)
        swapped = ((n_i // 32) % 4) * 128 + (n_i // 128) * 32 + n_i % 32
        perm[...] = (r_i == swapped).astype(F32).astype(BF16)
        eye[...] = (r_i == n_i).astype(F32).astype(BF16)

    def prepare_b():
        scopy.wait()
        sp[0:512] = s[0:512]
        for a in range(4):
            for b in range(4):
                to, at = 512 + a * 128 + b * 32, 512 + b * 128 + a * 32
                sp[to:to + 32] = s[at:at + 32]
        st[...] = s[...].astype(F32).T.astype(BF16)

    def prepare_c():
        h1copy.wait()
        hh, hl = split(h1[...])
        h1h[:, :512] = hh[:, :512]
        h1l[:, :512] = hl[:, :512]
        h1h[:, 512:] = dot(hh[:, 512:], perm[...]).astype(BF16)
        h1l[:, 512:] = dot(hl[:, 512:], perm[...]).astype(BF16)

    for op in ORDER:
        if op[0] < 3:
            step(op)
        elif op[0] == 3:
            _, i, k = op
            if k == 0:
                if i == 0:
                    dcopy.wait()
                    acopy.wait()
                group_g(i)
            elif k < 3:
                group_f(i, k == 1)
            else:
                if i < 3:
                    reduce_core(i)
                if i > 0:
                    reduce_g(i - 1)
                if i in (1, 2):
                    reduce_f(i - 1)
        else:
            (prepare_a, prepare_b, prepare_c)[op[1]]()
    reduce_g(3)

    g = gown[...]
    gh, gl = split(g)
    gsb[c, x, z] = dot(gh, sp[...]) + dot(gl, sp[...])

    half = width // 2

    def gs_core(ref, k):
        return send(ref, ref, gs_send.at[k], gs_recv.at[k], core)

    g1 = []
    for d in (1, 3, 2):
        a = gsb.at[c, x, z, :, pl.ds(0, half)]
        b = gsb.at[c, x, z, :, pl.ds(half, half)]
        g1.append(send(a, a, gs_send.at[d - 1], gs_recv.at[d - 1], xdev(d)))
        g1.append(send(b, b, gs_send.at[3 + d - 1], gs_recv.at[3 + d - 1], zdev(d)))

    reduce_core(3)

    at_diag = c * 512 + (x + c * (z - x)) * 128 + (z + c * (x - z)) * 32
    lane = lax.broadcasted_iota(jnp.int32, g.shape, 1)
    row = lax.broadcasted_iota(jnp.int32, g.shape, 0)
    on = lane == at_diag + row
    gb[c, x, z] = jnp.where(on, 0.0, g).astype(BF16)
    dg[c, x, z] = jnp.broadcast_to(jnp.sum(jnp.where(on, g, 0.0), axis=1, keepdims=True), (32, 128))

    wait_all(g1)
    g2 = []
    for d in (1, 3, 2):
        a = gsb.at[c, :, z, :, pl.ds(0, half)]
        b = gsb.at[c, x, :, :, pl.ds(half, half)]
        g2.append((d, 0, send(a, a, gs_send.at[6 + d - 1], gs_recv.at[6 + d - 1], zdev(d))))
        g2.append((d, 1, send(b, b, gs_send.at[9 + d - 1], gs_recv.at[9 + d - 1], xdev(d))))
    g3 = [
        gs_core(gsb.at[c, :, z, :, pl.ds(0, half)], 12),
        gs_core(gsb.at[c, x, :, :, pl.ds(half, half)], 13),
    ]
    gg1 = []
    for d in (1, 3, 2):
        a = gb.at[c, x, z, :, pl.ds(0, 512)]
        b = gb.at[c, x, z, :, pl.ds(512, 512)]
        e = dg.at[c, x, z]
        gg1.append(send(a, a, gg_send.at[d - 1], gg_recv.at[d - 1], xdev(d)))
        gg1.append(send(b, b, gg_send.at[3 + d - 1], gg_recv.at[3 + d - 1], zdev(d)))
        gg1.append(send(e, e, dg_send.at[d - 1], dg_recv.at[d - 1], xdev(d)))
    reduce_f(2)
    for d, o, cp in g2:
        cp.wait_recv()
        if o == 0:
            g3.append(gs_core(gsb.at[c, :, (z + 4 - d) % 4, :, pl.ds(0, half)], 14 + d))
        else:
            g3.append(gs_core(gsb.at[c, (x + 4 - d) % 4, :, :, pl.ds(half, half)], 17 + d))
    reduce_f(3)
    fn[:, :512] = fp[:, :512]
    fn[:, 512:] = dot(fp[:, 512:], perm[...]).astype(BF16)
    ft[:512] = dot(eye[...], fp[:, :512], NT).astype(BF16)
    ft[512:] = dot(perm[...], fp[:, 512:], NT).astype(BF16)
    proj = dot(fp[...], sp[...])
    wait_all(gg1)
    gg2 = []
    for d in (1, 3, 2):
        a = gb.at[c, :, z, :, pl.ds(0, 512)]
        b = gb.at[c, x, :, :, pl.ds(512, 512)]
        e = dg.at[c, :, z]
        gg2.append(send(a, a, gg_send.at[6 + d - 1], gg_recv.at[6 + d - 1], zdev(d)))
        gg2.append(send(b, b, gg_send.at[9 + d - 1], gg_recv.at[9 + d - 1], xdev(d)))
        gg2.append(send(e, e, dg_send.at[3 + d - 1], dg_recv.at[3 + d - 1], zdev(d)))
    h2copy.wait()
    wait_all(g3)

    gs = gsb[...].reshape(1024, width)
    gsh, gsl = split(gs)
    inner = dot(st[...], gsh) + dot(st[...], gsl)
    ip, im = pos_neg(inner)
    h2v = h2[...]
    h2s = split(h2v)
    num = jnp.maximum(proj, 0.0) + dot3(h2s, im)
    den = jnp.maximum(-proj, 0.0) + dot3(h2s, ip)
    second_v[...] = h2v * jnp.sqrt(num / den)
    second_copy = pltpu.make_async_copy(second_v, second_hbm, local_sem.at[5])
    second_copy.start()

    def grad_body(j, carry):
        sn = split(second_v[...])
        rows = gsb[j // 2, pl.ds((j % 2) * 2, 2)].reshape(256, width)
        res = dot3(split(rows), sn, NT) - ft[pl.ds(pl.multiple_of(j * 256, 256), 256), :].astype(F32)
        gr = dot3(split(res), sn)
        gp[0, j // 2, pl.ds((j % 2) * 2, 2)] = gr[:, :128].reshape(2, 4, 32, 128)
        gp[1, j // 2, pl.ds((j % 2) * 2, 2)] = gr[:, 128:].reshape(2, 4, 32, 128)
        return carry

    lax.fori_loop(0, 4, grad_body, 0)
    k1 = send(gp.at[1 - c], rcgp, rs_send.at[0], rs_recv.at[0], core)

    def first_body(j, carry):
        gt = gb[j // 2, pl.ds((j % 2) * 2, 2)].reshape(256, 1024)
        diag = dg[j // 2, pl.ds((j % 2) * 2, 2)].reshape(256, 128).T[0:1]
        gpos, gneg = jnp.maximum(gt, 0), jnp.maximum(-gt, 0)
        cols = pl.ds(pl.multiple_of(j * 256, 256), 256)
        f = fn[:, cols].astype(F32)
        h = h1[:, cols]
        num_ = jnp.maximum(f, 0.0) + (dot(h1h[...], gneg, NT) + dot(h1l[...], gneg, NT))
        den_ = jnp.maximum(-f, 0.0) + (dot(h1h[...], gpos, NT) + dot(h1l[...], gpos, NT)) + h * diag
        first_v[:, cols] = h * jnp.sqrt(num_ / den_)
        return carry

    k1.wait_recv()
    gs1[...] = gp[c] + rcgp[...]
    k2 = []
    for d in (1, 3, 2):
        k2.append(send(gs1.at[0, (x + d) % 4], r1a.at[d - 1], rs_send.at[d], rs_recv.at[d], xdev(d)))
        k2.append(send(gs1.at[1, :, (z + d) % 4], r1b.at[d - 1], rs_send.at[3 + d], rs_recv.at[3 + d], zdev(d)))
    wait_all(gg2)
    gg3 = [
        send(gb.at[c], gb.at[c], gg_send.at[12], gg_recv.at[12], core),
        send(dg.at[c], dg.at[c], dg_send.at[6], dg_recv.at[6], core),
    ]
    late = pending[-8:]
    del pending[-8:]
    settle()
    pending.extend(late)
    wait_all(k2)
    ab2[0] = (gs1[0, x] + r1a[0]) + (r1a[1] + r1a[2])
    ab2[1] = (gs1[1, :, z] + r1b[0]) + (r1b[1] + r1b[2])
    k3 = []
    for d in (1, 3, 2):
        k3.append(send(ab2.at[0, (z + d) % 4], r2a.at[d - 1], rs_send.at[6 + d], rs_recv.at[6 + d], zdev(d)))
        k3.append(send(ab2.at[1, (x + d) % 4], r2b.at[d - 1], rs_send.at[9 + d], rs_recv.at[9 + d], xdev(d)))
    wait_all(gg3)
    lax.fori_loop(0, 2, first_body, 0)
    wait_all(k3)
    ab3[0] = (ab2[0, z] + r2a[0]) + (r2a[1] + r2a[2])
    ab3[1] = (ab2[1, x] + r2b[0]) + (r2b[1] + r2b[2])
    k4 = []
    for d in (1, 3, 2):
        k4.append(send(ab3, r3.at[d - 1], rs_send.at[12 + d], rs_recv.at[12 + d], ydev(d)))
    lax.fori_loop(2, 4, first_body, 0)
    first_copy = pltpu.make_async_copy(first_v, first_hbm, local_sem.at[7])
    first_copy.start()
    wait_all(k4)
    fin[...] = (ab3[...] + r3[0]) + (r3[1] + r3[2])

    sq = fin[0] * fin[0] + fin[1] * fin[1]
    nrm[0] = (sq[0:8] + sq[8:16]) + (sq[16:24] + sq[24:32])
    n1 = []
    for dx in range(4):
        for dz in range(4):
            k = dx * 4 + dz - 1
            if k >= 0:
                n1.append(send(nrm.at[0], nrr.at[k], no_send.at[k], no_recv.at[k], plane(dx, dz)))
    dirh[c] = fin[yh]
    k5 = send(dirh.at[c], dirh.at[c], rs_send.at[16], rs_recv.at[16], core)
    wait_all(n1)
    nrm[1] = nrm[0] + jnp.sum(nrr[...], axis=0)
    n4 = send(nrm.at[1], nrc, no_send.at[15], no_recv.at[15], core)
    settle()
    k5.wait_recv()
    n4.wait_recv()
    total = jnp.sum(nrm[1] + nrc[...])
    scale = jnp.sqrt(total / (1024 * width) + 1e-06)
    dirf[:, :128] = dirh[0] / scale
    dirf[:, 128:] = dirh[1] / scale
    dir_copy = pltpu.make_async_copy(dirf, dir_hbm, local_sem.at[6])
    dir_copy.start()
    second_copy.wait()
    first_copy.wait()
    dir_copy.wait()


def shards(activations, dictionary, second_factor, first_codes, second_codes):
    tokens, rows = activations.shape
    sub, k1 = first_codes.shape[2:]
    k2 = second_codes.shape[3]
    v, dma = pltpu.VMEM, pltpu.SemaphoreType.DMA
    scratch = [
        v((2, 2, sub, rows), BF16), v((32, 32, rows), BF16), v((k1, k2), BF16), v((sub, k1), F32), v((sub, k2), F32),
        v((4, 2, 2, sub, 256), F32), v((4, 2, 32, 256), F32),
        v((4, 2, sub, 256), F32), v((4, 3, 32, 256), F32),
        v((4, sub, 256), F32), v((4, sub, 256), F32),
        v((sub, k1), BF16), v((32, k1), F32), v((k1, k2), BF16), v((k2, k1), BF16),
        v((512, 512), BF16), v((512, 512), BF16), v((sub, k1), BF16), v((sub, k1), BF16),
        v((sub, k1), BF16), v((k1, sub), BF16),
        v((2, 4, 4, 32, k2), F32), v((2, 4, 4, 32, k1), BF16), v((2, 4, 4, 32, 128), F32),
        v((sub, k1), F32), v((sub, k2), F32),
        v((2, 2, 4, 4, 32, 128), F32), v((2, 4, 4, 32, 128), F32), v((2, 4, 4, 32, 128), F32),
        v((3, 4, 32, 128), F32), v((3, 4, 32, 128), F32), v((2, 4, 32, 128), F32),
        v((3, 32, 128), F32), v((3, 32, 128), F32), v((2, 32, 128), F32), v((3, 2, 32, 128), F32),
        v((2, 32, 128), F32), v((2, 32, 128), F32), v((32, 256), F32),
        v((2, 8, 128), F32), v((15, 8, 128), F32), v((8, 128), F32),
        dma((8,)), dma((3, 30)), dma((3, 30)), dma((4, 5)), dma((4, 5)), dma((21,)), dma((21,)), dma((13,)), dma((13,)),
        dma((7,)), dma((7,)), dma((17,)), dma((17,)), dma((16,)), dma((16,)),
    ]
    hbm = pl.BlockSpec(memory_space=pl.ANY)
    first, second, direction = pl.pallas_call(
        kernel,
        out_shape=(
            jax.ShapeDtypeStruct((sub, k1), F32),
            jax.ShapeDtypeStruct((sub, k2), F32),
            jax.ShapeDtypeStruct((32, k2), F32),
        ),
        in_specs=[hbm] * 5,
        out_specs=(hbm,) * 3,
        scratch_shapes=scratch,
        compiler_params=pltpu.CompilerParams(
            collective_id=0, has_side_effects=True, vmem_limit_bytes=60 * 1024 * 1024
        ),
        name="sweep",
    )(activations.reshape(2, 2, sub, rows), dictionary.T, second_factor, first_codes.reshape(sub, k1), second_codes.reshape(sub, k2))
    return first.reshape(first_codes.shape), second.reshape(second_codes.shape), direction


def solution(mesh):
    in_specs = (
        P("tok", "hid"),
        P("hid", "tok"),
        P(),
        P("tok", "hid", None, None),
        P("tok", "hid", None, None),
    )
    out_specs = (P("tok", "hid", None, None), P("tok", "hid", None, None), P("tok", None))
    return jax.shard_map(shards, mesh=mesh, in_specs=in_specs, out_specs=out_specs, check_vma=False)
```

```python
import functools

import jax
import jax.numpy as jnp
from jax import lax
from jax.experimental import pallas as pl
from jax.experimental.pallas import tpu as pltpu
from jax.sharding import PartitionSpec as P

F32 = jnp.float32
BF16 = jnp.bfloat16
MESH = pl.DeviceIdType.MESH
NN = (((1,), (0,)), ((), ()))
NT = (((1,), (1,)), ((), ()))


def dot(a, b, dims=NN):
    return lax.dot_general(a, b, dims, preferred_element_type=F32)


def split(a):
    hi = a.astype(BF16)
    return hi, (a - hi.astype(F32)).astype(BF16)


def dot3(a, b, dims=NN):
    ah, al = a
    bh, bl = b
    return dot(ah, bh, dims) + (dot(al, bh, dims) + dot(ah, bl, dims))


def pos_neg(g):
    p = split(jnp.maximum(g, 0.0))
    n = split(jnp.maximum(-g, 0.0))
    return p, n


ORDER = (
    (2, 0), (0, 1, 1, 1), (0, 2, 0, 1, 0), (0, 1, 1, 0), (0, 2, 0, 0, 0), (0, 2, 0, 1, 1), (0, 2, 0, 0, 1),
    (0, 1, 0, 0), (2, 1), (0, 1, 0, 1), (4, 0), (4, 1), (1, 1, 0, 0), (1, 2, 0, 1, 0), (1, 1, 1, 0), (1, 2, 0, 0, 0),
    (1, 1, 0, 1), (1, 1, 1, 1), (1, 2, 0, 1, 1), (1, 2, 0, 0, 1), (0, 1, 2, 0), (0, 1, 2, 1), (0, 2, 1, 0, 1),
    (0, 2, 0, 2, 1), (0, 2, 1, 0, 0), (1, 2, 1, 0, 0), (0, 2, 0, 2, 0), (0, 2, 1, 1, 1), (1, 2, 1, 1, 1),
    (1, 2, 0, 2, 0), (1, 2, 0, 2, 1), (1, 2, 1, 0, 1), (1, 1, 2, 1), (0, 2, 2, 1, 1), (1, 1, 2, 0), (1, 2, 2, 1, 1),
    (0, 2, 2, 0, 0), (0, 2, 1, 1, 0), (0, 2, 1, 2, 1), (0, 2, 2, 1, 0), (0, 2, 3, 1, 1), (1, 2, 2, 0, 0), (4, 2),
    (1, 2, 1, 2, 1), (0, 2, 1, 2, 0), (3, 0, 0), (0, 2, 3, 0, 0), (1, 2, 1, 2, 0), (1, 2, 1, 1, 0), (3, 0, 1),
    (1, 2, 2, 0, 1), (1, 2, 3, 1, 1), (1, 2, 2, 2, 1), (0, 2, 2, 2, 1), (3, 0, 2), (3, 0, 3), (1, 2, 3, 0, 0),
    (0, 2, 2, 2, 0), (1, 2, 2, 1, 0), (0, 2, 2, 0, 1), (1, 2, 2, 2, 0), (3, 1, 0), (3, 1, 1), (0, 2, 3, 1, 0),
    (0, 2, 3, 0, 1), (0, 2, 3, 2, 0), (3, 1, 2), (1, 2, 3, 0, 1), (1, 2, 3, 2, 1), (3, 1, 3), (1, 2, 3, 1, 0),
    (0, 2, 3, 2, 1), (1, 2, 3, 2, 0), (3, 2, 0), (3, 2, 1), (3, 2, 2), (3, 3, 0), (3, 2, 3), (3, 3, 1), (3, 3, 2),
)


def kernel(
    act_hbm, dt_hbm, s_hbm, h1_hbm, h2_hbm,
    first_hbm, second_hbm, dir_hbm,
    act, w, s, h1, h2,
    pl_f, pl_g, rc_f, rc_g, ys_f, ry_f,
    fp, gown, sp, st, perm, eye, h1h, h1l, fn, ft,
    gsb, gb, dg, first_v, second_v, proj,
    gp, rcgp, gs1, r1a, r1b, ab2, r2a, r2b, ab3, r3, fin, dirh, dirf,
    nrm, nrr, nrc,
    local_sem, ga_send, ga_recv, fe_send, fe_recv, gs_send, gs_recv, gg_send, gg_recv,
    dg_send, dg_recv, rs_send, rs_recv, no_send, no_recv,
):
    hid = lax.axis_index("hid")
    tok = lax.axis_index("tok")
    yl, c = hid // 2, hid % 2
    yh, x, z = tok // 16, (tok // 4) % 4, tok % 4
    y = yh * 2 + yl
    sub = h1.shape[0]
    width = h2.shape[1]

    def dev(yl_, c_, yh_, x_, z_):
        return (yl_ * 2 + c_, yh_ * 16 + x_ * 4 + z_)

    core = dev(yl, 1 - c, yh, x, z)
    ylp = dev(1 - yl, c, yh, x, z)
    ylc = dev(1 - yl, 1 - c, yh, x, z)
    yhp = dev(yl, c, 1 - yh, x, z)

    def plane(dx, dz):
        return dev(yl, c, yh, (x + dx) % 4, (z + dz) % 4)

    def xdev(d):
        return plane(d, 0)

    def zdev(d):
        return plane(0, d)

    def ydev(d):
        yy = (y + d) % 4
        return dev(yy % 2, c, yy // 2, x, z)

    own_b = yh * 16 + x * 4 + z
    dcopy = pltpu.make_async_copy(dt_hbm, w.at[own_b], local_sem.at[1])
    dcopy.start()
    scopy = pltpu.make_async_copy(s_hbm, s, local_sem.at[2])
    scopy.start()
    h1copy = pltpu.make_async_copy(h1_hbm, h1, local_sem.at[3])
    h1copy.start()
    h2copy = pltpu.make_async_copy(h2_hbm, h2, local_sem.at[4])
    h2copy.start()
    acopy = pltpu.make_async_copy(act_hbm, act, local_sem.at[0])
    acopy.start()

    barrier = pltpu.get_barrier_semaphore()
    peers = [plane(dx, dz) for dx in range(4) for dz in range(4) if dx + dz > 0]
    peers += [ydev(1), ydev(2), ydev(3), core, ylc]
    for who in peers:
        pl.semaphore_signal(barrier, inc=1, device_id=who, device_id_type=MESH)
    pl.semaphore_wait(barrier, len(peers))

    pending = []

    def send(src, dst, ss, rs, who):
        cp = pltpu.make_async_remote_copy(
            src_ref=src, dst_ref=dst, send_sem=ss, recv_sem=rs, device_id=who, device_id_type=MESH
        )
        cp.start()
        pending.append(cp)
        return cp

    def settle():
        for cp in pending:
            cp.wait_send()
        pending.clear()

    def wait_all(cps):
        for cp in cps:
            cp.wait_recv()

    def part(o):
        p = (yh + o) % 2
        u = x + p * (z - x)
        v = z + p * (x - z)
        return p, u, v

    def blk(p, u_, v_):
        return p * 16 + u_ * (4 - 3 * p) + v_ * (1 + 3 * p)

    DU = (0, 3, 1, 2)

    def gdev(o, du, dv):
        p, u, v = part(o)
        u_, v_ = (u + du) % 4, (v + dv) % 4
        return (hid, yh * 16 + u_ * (4 - 3 * p) + v_ * (1 + 3 * p))

    def gblk(o, du, dv):
        p, u, v = part(o)
        return blk(p, (u + du) % 4, (v + dv) % 4)

    gd = {}
    arrived = set()

    def need(*key):
        if key not in arrived:
            arrived.add(key)
            gd[key].wait_recv()

    def gsend(key, k, b, who, r, hbm=False):
        o = key[0]
        dst = w.at[b, pl.ds(16 * r, 16)]
        src = dt_hbm.at[pl.ds(16 * r, 16)] if hbm else dst
        gd[key] = send(src, dst, ga_send.at[o, k], ga_recv.at[o, k], who)

    def own_here(o, r):
        if o == 1:
            need(2, r)

    def step(key):
        o = key[0]
        if o == 2:
            gsend(key, key[1], own_b, yhp, key[1], True)
        elif key[1] == 1:
            _, _, sg, r = key
            if sg < 2:
                own_here(o, r)
                gsend(key, sg * 2 + r, gblk(o, 0, 0), gdev(o, 3 if sg else 1, 0), r, o == 0)
            else:
                need(o, 1, r, r)
                gsend(key, 4 + r, gblk(o, 1 if r else 3, 0), gdev(o, 3 if r else 1, 0), r)
        else:
            _, _, i, sg, r = key
            k = 6 + 6 * i
            if sg < 2:
                if i == 0:
                    own_here(o, r)
                elif i < 3:
                    need(o, 1, i - 1, r)
                else:
                    need(o, 1, 2, r)
                gsend(key, k + sg * 2 + r, gblk(o, DU[i], 0), gdev(o, 0, 3 if sg else 1), r, o == 0 and i == 0)
            else:
                need(o, 2, i, r, r)
                gsend(key, k + 4 + r, gblk(o, DU[i], 1 if r else 3), gdev(o, 0, 3 if r else 1), r)

    def need_group(i):
        for o in (0, 1):
            for r in (0, 1):
                own_here(o, r)
                if i in (1, 2):
                    need(o, 1, i - 1, r)
                if i == 3:
                    need(o, 1, 2, r)
                for sg in (0, 1, 2):
                    need(o, 2, i, sg, r)

    fd = {}

    def chunk_of(o, i):
        p, u, v = part(o)
        return p * 4 + (u + DU[i]) % 4

    def weights(i):
        rows = []
        for o in (0, 1):
            p, u, v = part(o)
            rows += [w[blk(p, (u + DU[i]) % 4, j)] for j in range(4)]
        return jnp.concatenate(rows, axis=0)

    def group_g(i):
        need_group(i)
        lrows = jnp.concatenate([w[x * 4 + z], w[16 + x * 4 + z]], axis=0)
        g = dot(lrows, weights(i), NT)
        pl_g[i] = g.reshape(2, 32, g.shape[1])
        fd[i, 0] = send(pl_g.at[i, 1 - c], rc_g.at[i, 0], fe_send.at[i, 0], fe_recv.at[i, 0], core)
        fd[i, 1] = send(pl_g.at[i, c], rc_g.at[i, 1], fe_send.at[i, 1], fe_recv.at[i, 1], ylp)
        fd[i, 2] = send(pl_g.at[i, 1 - c], rc_g.at[i, 2], fe_send.at[i, 2], fe_recv.at[i, 2], ylc)

    def group_f(i, other):
        cc = 1 - c if other else c
        a = act[:, cc].reshape(2 * sub, act.shape[3])
        pl_f[i, cc] = dot(a, weights(i), NT).reshape(2, sub, 256)
        if other:
            fd[i, 3] = send(pl_f.at[i, cc], rc_f.at[i], fe_send.at[i, 3], fe_recv.at[i, 3], core)

    def reduce_core(i):
        fd[i, 3].wait_recv()
        ys_f[i] = pl_f[i, c, 1 - yl] + rc_f[i, 1 - yl]
        fd[i, 4] = send(ys_f.at[i], ry_f.at[i], fe_send.at[i, 4], fe_recv.at[i, 4], ylp)

    def lanes(q):
        return pl.ds(pl.multiple_of(q * 128, 128), 128)

    def reduce_g(i):
        for k in range(3):
            fd[i, k].wait_recv()
        g = (pl_g[i, c] + rc_g[i, 0]) + (rc_g[i, 1] + rc_g[i, 2])
        gown[:, lanes(chunk_of(0, i))] = g[:, :128]
        gown[:, lanes(chunk_of(1, i))] = g[:, 128:]

    def reduce_f(i):
        fd[i, 4].wait_recv()
        f = ((pl_f[i, c, yl] + rc_f[i, yl]) + ry_f[i]).astype(BF16)
        total = None
        for o in (0, 1):
            p, u, v = part(o)
            ui = (u + DU[i]) % 4
            q = p * 4 + ui
            fo = f[:, 128 * o:128 * o + 128]
            fp[:, lanes(q)] = fo
            term = dot(fo, sp[lanes(q), :])
            total = term if total is None else total + term
            turned = dot(eye[...], fo, NT).astype(BF16)
            for j in range(4):
                at = p * 512 + ui * (128 - 96 * p) + j * (32 + 96 * p)
                ft[pl.ds(pl.multiple_of(at, 32), 32), :] = turned[j * 32:j * 32 + 32]
        proj[...] = total if i == 0 else proj[...] + total

    def prepare_a():
        n_i = lax.broadcasted_iota(jnp.int32, (512, 512), 0)
        r_i = lax.broadcasted_iota(jnp.int32, (512, 512), 1)
        swapped = ((n_i // 32) % 4) * 128 + (n_i // 128) * 32 + n_i % 32
        perm[...] = (r_i == swapped).astype(F32).astype(BF16)
        eye[...] = (r_i == n_i)[:128, :128].astype(F32).astype(BF16)

    def prepare_b():
        scopy.wait()
        sp[0:512] = s[0:512]
        for a in range(4):
            for b in range(4):
                to, at = 512 + a * 128 + b * 32, 512 + b * 128 + a * 32
                sp[to:to + 32] = s[at:at + 32]
        st[...] = s[...].astype(F32).T.astype(BF16)

    def prepare_c():
        h1copy.wait()
        hh, hl = split(h1[...])
        h1h[:, :512] = hh[:, :512]
        h1l[:, :512] = hl[:, :512]
        h1h[:, 512:] = dot(hh[:, 512:], perm[...]).astype(BF16)
        h1l[:, 512:] = dot(hl[:, 512:], perm[...]).astype(BF16)

    for op in ORDER:
        if op[0] < 3:
            step(op)
        elif op[0] == 3:
            _, i, k = op
            if k == 0:
                if i == 0:
                    dcopy.wait()
                    acopy.wait()
                group_g(i)
            elif k < 3:
                group_f(i, k == 1)
            else:
                reduce_core(i)
                if i > 0:
                    reduce_g(i - 1)
                    reduce_f(i - 1)
        else:
            (prepare_a, prepare_b, prepare_c)[op[1]]()
    reduce_g(2)
    reduce_g(3)

    g = gown[...]
    gh, gl = split(g)
    gsb[c, x, z] = dot(gh, sp[...]) + dot(gl, sp[...])

    half = width // 2

    def gs_part(o, bx, bz):
        return gsb.at[c, bx, bz, :, pl.ds(half * o, half)]

    def gs_go(ref, k, who):
        return send(ref, ref, gs_send.at[k], gs_recv.at[k], who)

    g1 = {}
    for d in (1, 3, 2):
        g1[0, d] = gs_go(gs_part(0, x, z), d - 1, xdev(d))
        g1[1, d] = gs_go(gs_part(1, x, z), 2 + d, zdev(d))
    g2 = {}
    for d in (1, 3, 2):
        g2[0, 0, d] = gs_go(gs_part(0, x, z), 5 + d, zdev(d))
        g2[1, 0, d] = gs_go(gs_part(1, x, z), 17 + d, xdev(d))
    reduce_core(3)

    at_diag = c * 512 + (x + c * (z - x)) * 128 + (z + c * (x - z)) * 32
    lane = lax.broadcasted_iota(jnp.int32, g.shape, 1)
    row = lax.broadcasted_iota(jnp.int32, g.shape, 0)
    on = lane == at_diag + row
    gb[c, x, z] = jnp.where(on, 0.0, g).astype(BF16)
    dg[c, x, z] = jnp.broadcast_to(jnp.sum(jnp.where(on, g, 0.0), axis=1, keepdims=True), (32, 128))

    for j in (1, 3, 2):
        for o in (0, 1):
            g1[o, j].wait_recv()
            for d in (1, 3, 2):
                ref = gs_part(o, (x + 4 - j) % 4, z) if o == 0 else gs_part(o, x, (z + 4 - j) % 4)
                g2[o, j, d] = gs_go(ref, 5 + 12 * o + 3 * j + d, zdev(d) if o == 0 else xdev(d))
    g3 = [
        gs_go(gsb.at[c, :, z, :, pl.ds(0, half)], 30, core),
        gs_go(gsb.at[c, x, :, :, pl.ds(half, half)], 34, core),
    ]
    gg1 = []
    for d in (1, 3, 2):
        a = gb.at[c, x, z, :, pl.ds(0, 512)]
        b = gb.at[c, x, z, :, pl.ds(512, 512)]
        e = dg.at[c, x, z]
        gg1.append(send(a, a, gg_send.at[d - 1], gg_recv.at[d - 1], xdev(d)))
        gg1.append(send(b, b, gg_send.at[3 + d - 1], gg_recv.at[3 + d - 1], zdev(d)))
        gg1.append(send(e, e, dg_send.at[d - 1], dg_recv.at[d - 1], xdev(d)))
    reduce_f(2)
    for d in (1, 3, 2):
        for o in (0, 1):
            for j in (0, 1, 3, 2):
                g2[o, j, d].wait_recv()
            if o == 0:
                ref = gsb.at[c, :, (z + 4 - d) % 4, :, pl.ds(0, half)]
            else:
                ref = gsb.at[c, (x + 4 - d) % 4, :, :, pl.ds(half, half)]
            g3.append(gs_go(ref, 30 + 4 * o + d, core))
    wait_all(gg1)
    gg2 = []
    for d in (1, 3, 2):
        a = gb.at[c, :, z, :, pl.ds(0, 512)]
        b = gb.at[c, x, :, :, pl.ds(512, 512)]
        e = dg.at[c, :, z]
        gg2.append(send(a, a, gg_send.at[6 + d - 1], gg_recv.at[6 + d - 1], zdev(d)))
        gg2.append(send(b, b, gg_send.at[9 + d - 1], gg_recv.at[9 + d - 1], xdev(d)))
        gg2.append(send(e, e, dg_send.at[3 + d - 1], dg_recv.at[3 + d - 1], zdev(d)))
    h2copy.wait()
    reduce_f(3)
    wait_all(g3)

    gs = gsb[...].reshape(1024, width)
    gsh, gsl = split(gs)
    inner = dot(st[...], gsh) + dot(st[...], gsl)
    ip, im = pos_neg(inner)
    h2v = h2[...]
    h2s = split(h2v)
    pr = proj[...]
    num = jnp.maximum(pr, 0.0) + dot3(h2s, im)
    den = jnp.maximum(-pr, 0.0) + dot3(h2s, ip)
    second = h2v * jnp.sqrt(num / den)
    second_v[...] = second
    second_copy = pltpu.make_async_copy(second_v, second_hbm, local_sem.at[5])
    second_copy.start()

    sn = split(second)
    k1 = []
    for p in (0, 1):
        rows = slice(512 * p, 512 * p + 512)
        res = dot3((gsh[rows], gsl[rows]), sn, NT) - ft[rows, :].astype(F32)
        gr = dot3(split(res), sn)
        gp[0, p] = gr[:, :128].reshape(4, 4, 32, 128)
        gp[1, p] = gr[:, 128:].reshape(4, 4, 32, 128)
        k1.append(send(gp.at[1 - c, p], rcgp.at[p], rs_send.at[17 * p], rs_recv.at[17 * p], core))

    def first_body(j, carry):
        gt = gb[j // 2, pl.ds((j % 2) * 2, 2)].reshape(256, 1024)
        diag = dg[j // 2, pl.ds((j % 2) * 2, 2)].reshape(256, 128).T[0:1]
        gpos, gneg = jnp.maximum(gt, 0), jnp.maximum(-gt, 0)
        cols = pl.ds(pl.multiple_of(j * 256, 256), 256)
        f = fn[:, cols].astype(F32)
        h = h1[:, cols]
        num_ = jnp.maximum(f, 0.0) + (dot(h1h[...], gneg, NT) + dot(h1l[...], gneg, NT))
        den_ = jnp.maximum(-f, 0.0) + (dot(h1h[...], gpos, NT) + dot(h1l[...], gpos, NT)) + h * diag
        first_v[:, cols] = h * jnp.sqrt(num_ / den_)
        return carry

    k1[0].wait_recv()
    gs1[0] = gp[c, 0] + rcgp[0]
    k1[1].wait_recv()
    gs1[1] = gp[c, 1] + rcgp[1]
    k2 = []
    for d in (1, 3, 2):
        k2.append(send(gs1.at[0, (x + d) % 4], r1a.at[d - 1], rs_send.at[d], rs_recv.at[d], xdev(d)))
        k2.append(send(gs1.at[1, :, (z + d) % 4], r1b.at[d - 1], rs_send.at[3 + d], rs_recv.at[3 + d], zdev(d)))
    wait_all(gg2)
    gg3 = [
        send(gb.at[c], gb.at[c], gg_send.at[12], gg_recv.at[12], core),
        send(dg.at[c], dg.at[c], dg_send.at[6], dg_recv.at[6], core),
    ]
    late = pending[-8:]
    del pending[-8:]
    settle()
    pending.extend(late)
    fn[:, :512] = fp[:, :512]
    fn[:, 512:] = dot(fp[:, 512:], perm[...]).astype(BF16)
    wait_all(k2)
    ab2[0] = (gs1[0, x] + r1a[0]) + (r1a[1] + r1a[2])
    ab2[1] = (gs1[1, :, z] + r1b[0]) + (r1b[1] + r1b[2])
    k3 = []
    for d in (1, 3, 2):
        k3.append(send(ab2.at[0, (z + d) % 4], r2a.at[d - 1], rs_send.at[6 + d], rs_recv.at[6 + d], zdev(d)))
        k3.append(send(ab2.at[1, (x + d) % 4], r2b.at[d - 1], rs_send.at[9 + d], rs_recv.at[9 + d], xdev(d)))
    wait_all(gg3)
    lax.fori_loop(0, 2, first_body, 0)
    wait_all(k3)
    ab3[0] = (ab2[0, z] + r2a[0]) + (r2a[1] + r2a[2])
    ab3[1] = (ab2[1, x] + r2b[0]) + (r2b[1] + r2b[2])
    k4 = []
    for d in (1, 3, 2):
        k4.append(send(ab3, r3.at[d - 1], rs_send.at[12 + d], rs_recv.at[12 + d], ydev(d)))
    lax.fori_loop(2, 3, first_body, 0)
    settle()
    wait_all(k4)
    fin[...] = (ab3[...] + r3[0]) + (r3[1] + r3[2])

    sq = fin[0] * fin[0] + fin[1] * fin[1]
    nrm[0] = (sq[0:8] + sq[8:16]) + (sq[16:24] + sq[24:32])
    n1 = []
    for dx in range(4):
        for dz in range(4):
            k = dx * 4 + dz - 1
            if k >= 0:
                n1.append(send(nrm.at[0], nrr.at[k], no_send.at[k], no_recv.at[k], plane(dx, dz)))
    dirh[c] = fin[yh]
    k5 = send(dirh.at[c], dirh.at[c], rs_send.at[16], rs_recv.at[16], core)
    lax.fori_loop(3, 4, first_body, 0)
    first_copy = pltpu.make_async_copy(first_v, first_hbm, local_sem.at[7])
    first_copy.start()
    wait_all(n1)
    nrm[1] = nrm[0] + jnp.sum(nrr[...], axis=0)
    n4 = send(nrm.at[1], nrc, no_send.at[15], no_recv.at[15], core)
    settle()
    k5.wait_recv()
    n4.wait_recv()
    total = jnp.sum(jnp.sum(nrm[1] + nrc[...], axis=1, keepdims=True), axis=0, keepdims=True)
    scale = jnp.sqrt(total / (1024 * width) + 1e-06)
    dirf[:, :128] = dirh[0] / scale
    dirf[:, 128:] = dirh[1] / scale
    dir_copy = pltpu.make_async_copy(dirf, dir_hbm, local_sem.at[6])
    dir_copy.start()
    second_copy.wait()
    first_copy.wait()
    dir_copy.wait()


def hand_out(a, b, c, a_out, b_out, c_out, av, bv, cv, sem):
    loads = [pltpu.make_async_copy(src, held, sem.at[k]) for k, (src, held) in enumerate(((a, av), (b, bv), (c, cv)))]
    stores = [
        pltpu.make_async_copy(held, dst, sem.at[3 + k])
        for k, (held, dst) in enumerate(((av, a_out), (bv, b_out), (cv, c_out)))
    ]
    for cp in loads:
        cp.start()
    for load, store in zip(loads, stores):
        load.wait()
        store.start()
    for cp in stores:
        cp.wait()


def shards(activations, dictionary, second_factor, first_codes, second_codes):
    tokens, rows = activations.shape
    sub, k1 = first_codes.shape[2:]
    k2 = second_codes.shape[3]
    v, dma = pltpu.VMEM, pltpu.SemaphoreType.DMA
    scratch = [
        v((2, 2, sub, rows), BF16), v((32, 32, rows), BF16), v((k1, k2), BF16), v((sub, k1), F32), v((sub, k2), F32),
        v((4, 2, 2, sub, 256), F32), v((4, 2, 32, 256), F32),
        v((4, 2, sub, 256), F32), v((4, 3, 32, 256), F32),
        v((4, sub, 256), F32), v((4, sub, 256), F32),
        v((sub, k1), BF16), v((32, k1), F32), v((k1, k2), BF16), v((k2, k1), BF16),
        v((512, 512), BF16), v((128, 128), BF16), v((sub, k1), BF16), v((sub, k1), BF16),
        v((sub, k1), BF16), v((k1, sub), BF16),
        v((2, 4, 4, 32, k2), F32), v((2, 4, 4, 32, k1), BF16), v((2, 4, 4, 32, 128), F32),
        v((sub, k1), F32), v((sub, k2), F32), v((sub, k2), F32),
        v((2, 2, 4, 4, 32, 128), F32), v((2, 4, 4, 32, 128), F32), v((2, 4, 4, 32, 128), F32),
        v((3, 4, 32, 128), F32), v((3, 4, 32, 128), F32), v((2, 4, 32, 128), F32),
        v((3, 32, 128), F32), v((3, 32, 128), F32), v((2, 32, 128), F32), v((3, 2, 32, 128), F32),
        v((2, 32, 128), F32), v((2, 32, 128), F32), v((32, 256), F32),
        v((2, 8, 128), F32), v((15, 8, 128), F32), v((8, 128), F32),
        dma((8,)), dma((3, 30)), dma((3, 30)), dma((4, 5)), dma((4, 5)), dma((38,)), dma((38,)), dma((13,)), dma((13,)),
        dma((7,)), dma((7,)), dma((18,)), dma((18,)), dma((16,)), dma((16,)),
    ]
    hbm = pl.BlockSpec(memory_space=pl.ANY)
    first, second, direction = pl.pallas_call(
        kernel,
        out_shape=(
            jax.ShapeDtypeStruct((sub, k1), F32),
            jax.ShapeDtypeStruct((sub, k2), F32),
            jax.ShapeDtypeStruct((32, k2), F32),
        ),
        in_specs=[hbm] * 5,
        out_specs=(hbm,) * 3,
        scratch_shapes=scratch,
        compiler_params=pltpu.CompilerParams(
            collective_id=0, has_side_effects=True, vmem_limit_bytes=60 * 1024 * 1024
        ),
        name="sweep",
    )(activations.reshape(2, 2, sub, rows), dictionary.T, second_factor, first_codes.reshape(sub, k1), second_codes.reshape(sub, k2))
    first, second, direction = pl.pallas_call(
        hand_out,
        out_shape=tuple(jax.ShapeDtypeStruct(o.shape, F32) for o in (first, second, direction)),
        in_specs=[hbm] * 3,
        out_specs=(hbm,) * 3,
        scratch_shapes=[v((sub, k1), F32), v((sub, k2), F32), v((32, k2), F32), dma((6,))],
        name="hand_out",
    )(first, second, direction)
    return first.reshape(first_codes.shape), second.reshape(second_codes.shape), direction


def solution(mesh):
    in_specs = (
        P("tok", "hid"),
        P("hid", "tok"),
        P(),
        P("tok", "hid", None, None),
        P("tok", "hid", None, None),
    )
    out_specs = (P("tok", "hid", None, None), P("tok", "hid", None, None), P("tok", None))
    return jax.shard_map(shards, mesh=mesh, in_specs=in_specs, out_specs=out_specs, check_vma=False)
```

```python
import functools

import jax
import jax.numpy as jnp
from jax import lax
from jax.experimental import pallas as pl
from jax.experimental.pallas import tpu as pltpu
from jax.sharding import PartitionSpec as P

F32 = jnp.float32
BF16 = jnp.bfloat16
MESH = pl.DeviceIdType.MESH
NN = (((1,), (0,)), ((), ()))
NT = (((1,), (1,)), ((), ()))


def dot(a, b, dims=NN):
    return lax.dot_general(a, b, dims, preferred_element_type=F32)


def split(a):
    hi = a.astype(BF16)
    return hi, (a - hi.astype(F32)).astype(BF16)


def dot3(a, b, dims=NN):
    ah, al = a
    bh, bl = b
    return dot(ah, bh, dims) + (dot(al, bh, dims) + dot(ah, bl, dims))


def pos_neg(g):
    p = split(jnp.maximum(g, 0.0))
    n = split(jnp.maximum(-g, 0.0))
    return p, n


ORDER = (
    (2, 0), (0, 2, 0, 1, 1), (0, 1, 1, 1), (0, 2, 0, 0, 0), (0, 1, 1, 0), (0, 2, 0, 1, 0), (0, 1, 0, 0),
    (0, 2, 0, 0, 1), (0, 1, 0, 1), (2, 1), (4, 0), (4, 1), (1, 1, 1, 0), (1, 2, 0, 0, 0), (0, 1, 2, 1), (1, 1, 0, 0),
    (1, 1, 0, 1), (0, 2, 0, 2, 1), (1, 2, 0, 0, 1), (1, 2, 0, 1, 0), (0, 1, 2, 0), (1, 1, 1, 1), (1, 2, 0, 1, 1),
    (0, 2, 0, 2, 0), (0, 2, 1, 0, 0), (0, 2, 2, 1, 1), (1, 1, 2, 0), (1, 2, 0, 2, 0), (1, 2, 1, 1, 0),
    (1, 2, 1, 0, 0), (1, 2, 2, 0, 0), (0, 2, 2, 0, 0), (1, 2, 1, 1, 1), (0, 2, 1, 1, 1), (1, 2, 0, 2, 1),
    (1, 1, 2, 1), (0, 2, 1, 1, 0), (1, 2, 2, 1, 1), (0, 2, 1, 2, 0), (1, 2, 1, 0, 1), (0, 2, 1, 2, 1),
    (0, 2, 2, 1, 0), (1, 2, 1, 2, 0), (1, 2, 3, 0, 0), (0, 2, 3, 1, 1), (0, 2, 1, 0, 1), (4, 2), (1, 2, 1, 2, 1),
    (0, 2, 3, 0, 0), (3, 0, 0), (1, 2, 2, 1, 0), (3, 0, 1), (0, 2, 2, 0, 1), (1, 2, 2, 0, 1), (0, 2, 2, 2, 1),
    (1, 2, 3, 1, 1), (1, 2, 2, 2, 1), (0, 2, 2, 2, 0), (3, 0, 2), (3, 0, 3), (1, 2, 2, 2, 0), (0, 2, 3, 1, 0),
    (3, 1, 0), (0, 2, 3, 0, 1), (1, 2, 3, 0, 1), (1, 2, 3, 1, 0), (3, 1, 1), (3, 1, 2), (0, 2, 3, 2, 1),
    (1, 2, 3, 2, 0), (1, 2, 3, 2, 1), (0, 2, 3, 2, 0), (3, 1, 3), (3, 2, 0), (3, 2, 1), (3, 2, 2), (3, 0, 4), (3, 3, 0),
    (3, 2, 3), (3, 3, 1),
)


def kernel(
    act_hbm, dt_hbm, s_hbm, h1_hbm, h2_hbm,
    first_hbm, second_hbm, dir_hbm,
    act, w, s, h1, h2,
    pl_f, pl_g, rc_f, rc_g, ys_f, ys_g, ry_f,
    fp, gown, sp, st, perm, eye, h1h, h1l, fn, ft,
    gsb, gb, dg, first_v, second_v, proj,
    gp, rcgp, gs1, r1a, r1b, ab2, r2a, r2b, ab3, r3, fin, dirh, dirf,
    nrm, nrr,
    local_sem, ga_send, ga_recv, fe_send, fe_recv, gs_send, gs_recv, gg_send, gg_recv,
    dg_send, dg_recv, rs_send, rs_recv, no_send, no_recv,
):
    hid = lax.axis_index("hid")
    tok = lax.axis_index("tok")
    yl, c = hid // 2, hid % 2
    yh, x, z = tok // 16, (tok // 4) % 4, tok % 4
    y = yh * 2 + yl
    sub = h1.shape[0]
    width = h2.shape[1]

    def dev(yl_, c_, yh_, x_, z_):
        return (yl_ * 2 + c_, yh_ * 16 + x_ * 4 + z_)

    core = dev(yl, 1 - c, yh, x, z)
    ylp = dev(1 - yl, c, yh, x, z)
    ylc = dev(1 - yl, 1 - c, yh, x, z)
    yhp = dev(yl, c, 1 - yh, x, z)

    def plane(dx, dz):
        return dev(yl, c, yh, (x + dx) % 4, (z + dz) % 4)

    def xdev(d):
        return plane(d, 0)

    def zdev(d):
        return plane(0, d)

    def ydev(d):
        yy = (y + d) % 4
        return dev(yy % 2, c, yy // 2, x, z)

    own_b = yh * 16 + x * 4 + z
    dcopy = pltpu.make_async_copy(dt_hbm, w.at[own_b], local_sem.at[1])
    dcopy.start()
    scopy = pltpu.make_async_copy(s_hbm, s, local_sem.at[2])
    scopy.start()
    h1copy = pltpu.make_async_copy(h1_hbm, h1, local_sem.at[3])
    h1copy.start()
    h2copy = pltpu.make_async_copy(h2_hbm, h2, local_sem.at[4])
    h2copy.start()
    acopy = pltpu.make_async_copy(act_hbm, act, local_sem.at[0])
    acopy.start()

    barrier = pltpu.get_barrier_semaphore()
    peers = [xdev(1), xdev(3), zdev(1), zdev(3), ydev(1), ydev(2), ydev(3), core, ylc]
    for who in peers:
        pl.semaphore_signal(barrier, inc=1, device_id=who, device_id_type=MESH)
    pl.semaphore_wait(barrier, len(peers))

    pending = []

    def send(src, dst, ss, rs, who):
        cp = pltpu.make_async_remote_copy(
            src_ref=src, dst_ref=dst, send_sem=ss, recv_sem=rs, device_id=who, device_id_type=MESH
        )
        cp.start()
        pending.append(cp)
        return cp

    def settle():
        for cp in pending:
            cp.wait_send()
        pending.clear()

    def wait_all(cps):
        for cp in cps:
            cp.wait_recv()

    def part(o):
        p = (yh + o) % 2
        u = x + p * (z - x)
        v = z + p * (x - z)
        return p, u, v

    def blk(p, u_, v_):
        return p * 16 + u_ * (4 - 3 * p) + v_ * (1 + 3 * p)

    DU = (0, 3, 1, 2)

    def gdev(o, du, dv):
        p, u, v = part(o)
        u_, v_ = (u + du) % 4, (v + dv) % 4
        return (hid, yh * 16 + u_ * (4 - 3 * p) + v_ * (1 + 3 * p))

    def gblk(o, du, dv):
        p, u, v = part(o)
        return blk(p, (u + du) % 4, (v + dv) % 4)

    gd = {}
    arrived = set()

    def need(*key):
        if key not in arrived:
            arrived.add(key)
            gd[key].wait_recv()

    def gsend(key, k, b, who, r, hbm=False):
        o = key[0]
        dst = w.at[b, pl.ds(16 * r, 16)]
        src = dt_hbm.at[pl.ds(16 * r, 16)] if hbm else dst
        gd[key] = send(src, dst, ga_send.at[o, k], ga_recv.at[o, k], who)

    def own_here(o, r):
        if o == 1:
            need(2, r)

    def step(key):
        o = key[0]
        if o == 2:
            gsend(key, key[1], own_b, yhp, key[1], True)
        elif key[1] == 1:
            _, _, sg, r = key
            if sg < 2:
                own_here(o, r)
                gsend(key, sg * 2 + r, gblk(o, 0, 0), gdev(o, 3 if sg else 1, 0), r, o == 0)
            else:
                need(o, 1, r, r)
                gsend(key, 4 + r, gblk(o, 1 if r else 3, 0), gdev(o, 3 if r else 1, 0), r)
        else:
            _, _, i, sg, r = key
            k = 6 + 6 * i
            if sg < 2:
                if i == 0:
                    own_here(o, r)
                elif i < 3:
                    need(o, 1, i - 1, r)
                else:
                    need(o, 1, 2, r)
                gsend(key, k + sg * 2 + r, gblk(o, DU[i], 0), gdev(o, 0, 3 if sg else 1), r, o == 0 and i == 0)
            else:
                need(o, 2, i, r, r)
                gsend(key, k + 4 + r, gblk(o, DU[i], 1 if r else 3), gdev(o, 0, 3 if r else 1), r)

    def need_group(i):
        for o in (0, 1):
            for r in (0, 1):
                own_here(o, r)
                if i in (1, 2):
                    need(o, 1, i - 1, r)
                if i == 3:
                    need(o, 1, 2, r)
                for sg in (0, 1, 2):
                    need(o, 2, i, sg, r)

    fd = {}

    def chunk_of(o, i):
        p, u, v = part(o)
        return p * 4 + (u + DU[i]) % 4

    def weights(i):
        rows = []
        for o in (0, 1):
            p, u, v = part(o)
            rows += [w[blk(p, (u + DU[i]) % 4, j)] for j in range(4)]
        return jnp.concatenate(rows, axis=0)

    def group_g(i):
        need_group(i)
        lrows = jnp.concatenate([w[x * 4 + z], w[16 + x * 4 + z]], axis=0)
        g = dot(lrows, weights(i), NT)
        pl_g[i] = g.reshape(2, 32, g.shape[1])
        fd[i, 0] = send(pl_g.at[i, 1 - c], rc_g.at[i, 0], fe_send.at[i, 0], fe_recv.at[i, 0], core)
        if i < 3:
            return
        fd[i, 1] = send(pl_g.at[i, c], rc_g.at[i, 1], fe_send.at[i, 1], fe_recv.at[i, 1], ylp)
        fd[i, 2] = send(pl_g.at[i, 1 - c], rc_g.at[i, 2], fe_send.at[i, 2], fe_recv.at[i, 2], ylc)

    def group_f(i, other):
        cc = 1 - c if other else c
        a = act[:, cc].reshape(2 * sub, act.shape[3])
        pl_f[i, cc] = dot(a, weights(i), NT).reshape(2, sub, 256)
        if other:
            fd[i, 3] = send(pl_f.at[i, cc], rc_f.at[i], fe_send.at[i, 3], fe_recv.at[i, 3], core)

    def reduce_core(i):
        if i < 3:
            fd[i, 0].wait_recv()
            ys_g[i] = pl_g[i, c] + rc_g[i, 0]
            fd[i, 1] = send(ys_g.at[i], rc_g.at[i, 1], fe_send.at[i, 1], fe_recv.at[i, 1], ylp)
        fd[i, 3].wait_recv()
        out, back = (ys_f.at[i], ry_f.at[i])
        out[...] = (pl_f[i, c, 1 - yl] + rc_f[i, 1 - yl]).astype(out.dtype)
        fd[i, 4] = send(out, back, fe_send.at[i, 4], fe_recv.at[i, 4], ylp)

    def lanes(q):
        return pl.ds(pl.multiple_of(q * 128, 128), 128)

    def reduce_g(i):
        if i < 3:
            fd[i, 1].wait_recv()
            g = ys_g[i] + rc_g[i, 1]
        else:
            for k in range(3):
                fd[i, k].wait_recv()
            g = (pl_g[i, c] + rc_g[i, 0]) + (rc_g[i, 1] + rc_g[i, 2])
        gown[:, lanes(chunk_of(0, i))] = g[:, :128]
        gown[:, lanes(chunk_of(1, i))] = g[:, 128:]

    def reduce_f(i):
        fd[i, 4].wait_recv()
        back = ry_f[i]
        f = ((pl_f[i, c, yl] + rc_f[i, yl]) + back).astype(BF16)
        total = None
        for o in (0, 1):
            p, u, v = part(o)
            ui = (u + DU[i]) % 4
            q = p * 4 + ui
            fo = f[:, 128 * o:128 * o + 128]
            fp[:, lanes(q)] = fo
            term = dot(fo, sp[lanes(q), :])
            total = term if total is None else total + term
            turned = dot(eye[...], fo, NT).astype(BF16)
            for j in range(4):
                at = p * 512 + ui * (128 - 96 * p) + j * (32 + 96 * p)
                ft[pl.ds(pl.multiple_of(at, 32), 32), :] = turned[j * 32:j * 32 + 32]
        proj[...] = total if i == 0 else proj[...] + total

    def prepare_a():
        n_i = lax.broadcasted_iota(jnp.int32, (512, 512), 0)
        r_i = lax.broadcasted_iota(jnp.int32, (512, 512), 1)
        swapped = ((n_i // 32) % 4) * 128 + (n_i // 128) * 32 + n_i % 32
        perm[...] = (r_i == swapped).astype(F32).astype(BF16)
        eye[...] = (r_i == n_i)[:128, :128].astype(F32).astype(BF16)

    def prepare_b():
        scopy.wait()
        sp[0:512] = s[0:512]
        for a in range(4):
            for b in range(4):
                to, at = 512 + a * 128 + b * 32, 512 + b * 128 + a * 32
                sp[to:to + 32] = s[at:at + 32]
        st[...] = s[...].astype(F32).T.astype(BF16)

    def prepare_c():
        h1copy.wait()
        hh, hl = split(h1[...])
        h1h[:, :512] = hh[:, :512]
        h1l[:, :512] = hl[:, :512]
        h1h[:, 512:] = dot(hh[:, 512:], perm[...]).astype(BF16)
        h1l[:, 512:] = dot(hl[:, 512:], perm[...]).astype(BF16)

    for op in ORDER:
        if op[0] < 3:
            step(op)
        elif op[0] == 3:
            _, i, k = op
            if k == 0:
                if i == 0:
                    dcopy.wait()
                    acopy.wait()
                group_g(i)
            elif k < 3:
                group_f(i, k == 1)
            elif k == 4:
                reduce_f(i)
            else:
                reduce_core(i)
                if i > 0:
                    reduce_g(i - 1)
        else:
            (prepare_a, prepare_b, prepare_c)[op[1]]()
    reduce_g(2)
    reduce_g(3)

    g = gown[...]
    gh, gl = split(g)
    gsb[c, x, z] = dot(gh, sp[...]) + dot(gl, sp[...])

    half = width // 2

    def gs_part(o, bx, bz):
        return gsb.at[c, bx, bz, :, pl.ds(half * o, half)]

    def gs_go(ref, k, who):
        return send(ref, ref, gs_send.at[k], gs_recv.at[k], who)

    g1 = {}
    for d in (1, 3, 2):
        g1[0, d] = gs_go(gs_part(0, x, z), d - 1, xdev(d))
        g1[1, d] = gs_go(gs_part(1, x, z), 2 + d, zdev(d))
    g2 = {}
    for d in (1, 3, 2):
        g2[0, 0, d] = gs_go(gs_part(0, x, z), 5 + d, zdev(d))
        g2[1, 0, d] = gs_go(gs_part(1, x, z), 17 + d, xdev(d))
    group_f(3, False)
    reduce_core(3)

    at_diag = c * 512 + (x + c * (z - x)) * 128 + (z + c * (x - z)) * 32
    lane = lax.broadcasted_iota(jnp.int32, g.shape, 1)
    row = lax.broadcasted_iota(jnp.int32, g.shape, 0)
    on = lane == at_diag + row
    reduce_f(1)
    gb[c, x, z] = jnp.where(on, 0.0, g).astype(BF16)
    dg[c, x, z] = jnp.broadcast_to(jnp.sum(jnp.where(on, g, 0.0), axis=1, keepdims=True), (32, 128))

    for j in (1, 3, 2):
        for o in (0, 1):
            g1[o, j].wait_recv()
            for d in (1, 3, 2):
                ref = gs_part(o, (x + 4 - j) % 4, z) if o == 0 else gs_part(o, x, (z + 4 - j) % 4)
                g2[o, j, d] = gs_go(ref, 5 + 12 * o + 3 * j + d, zdev(d) if o == 0 else xdev(d))
    g3 = [
        gs_go(gsb.at[c, :, z, :, pl.ds(0, half)], 30, core),
        gs_go(gsb.at[c, x, :, :, pl.ds(half, half)], 34, core),
    ]
    gg1 = []
    for d in (1, 3, 2):
        a = gb.at[c, x, z, :, pl.ds(0, 512)]
        b = gb.at[c, x, z, :, pl.ds(512, 512)]
        e = dg.at[c, x, z]
        gg1.append(send(a, a, gg_send.at[d - 1], gg_recv.at[d - 1], xdev(d)))
        gg1.append(send(b, b, gg_send.at[3 + d - 1], gg_recv.at[3 + d - 1], zdev(d)))
        gg1.append(send(e, e, dg_send.at[d - 1], dg_recv.at[d - 1], xdev(d)))
    wait_all(gg1)
    gg2 = []
    for d in (1, 3, 2):
        a = gb.at[c, :, z, :, pl.ds(0, 512)]
        b = gb.at[c, x, :, :, pl.ds(512, 512)]
        e = dg.at[c, :, z]
        gg2.append(send(a, a, gg_send.at[6 + d - 1], gg_recv.at[6 + d - 1], zdev(d)))
        gg2.append(send(b, b, gg_send.at[9 + d - 1], gg_recv.at[9 + d - 1], xdev(d)))
        gg2.append(send(e, e, dg_send.at[3 + d - 1], dg_recv.at[3 + d - 1], zdev(d)))
    for d in (1, 3, 2):
        for o in (0, 1):
            for j in (0, 1, 3, 2):
                g2[o, j, d].wait_recv()
            if o == 0:
                ref = gsb.at[c, :, (z + 4 - d) % 4, :, pl.ds(0, half)]
            else:
                ref = gsb.at[c, (x + 4 - d) % 4, :, :, pl.ds(half, half)]
            g3.append(gs_go(ref, 30 + 4 * o + d, core))
    reduce_f(2)
    h2copy.wait()
    reduce_f(3)
    wait_all(g3)

    gs = gsb[...].reshape(1024, width)
    gsh, gsl = split(gs)
    inner = dot(st[...], gsh) + dot(st[...], gsl)
    ip, im = pos_neg(inner)
    h2v = h2[...]
    h2s = split(h2v)
    pr = proj[...]
    num = jnp.maximum(pr, 0.0) + dot3(h2s, im)
    den = jnp.maximum(-pr, 0.0) + dot3(h2s, ip)
    second = h2v * jnp.sqrt(num / den)
    second_v[...] = second
    second_copy = pltpu.make_async_copy(second_v, second_hbm, local_sem.at[5])
    second_copy.start()

    sn = split(second)
    k1 = []
    for p in (0, 1):
        rows = slice(512 * p, 512 * p + 512)
        res = dot3((gsh[rows], gsl[rows]), sn, NT) - ft[rows, :].astype(F32)
        gr = dot3(split(res), sn)
        gp[0, p] = gr[:, :128].reshape(4, 4, 32, 128)
        gp[1, p] = gr[:, 128:].reshape(4, 4, 32, 128)
        k1.append(send(gp.at[1 - c, p], rcgp.at[p], rs_send.at[17 * p], rs_recv.at[17 * p], core))

    def first_body(j, carry):
        gt = gb[j // 2, pl.ds((j % 2) * 2, 2)].reshape(256, 1024)
        diag = dg[j // 2, pl.ds((j % 2) * 2, 2)].reshape(256, 128).T[0:1]
        gpos, gneg = jnp.maximum(gt, 0), jnp.maximum(-gt, 0)
        cols = pl.ds(pl.multiple_of(j * 256, 256), 256)
        f = fn[:, cols].astype(F32)
        h = h1[:, cols]
        num_ = jnp.maximum(f, 0.0) + (dot(h1h[...], gneg, NT) + dot(h1l[...], gneg, NT))
        den_ = jnp.maximum(-f, 0.0) + (dot(h1h[...], gpos, NT) + dot(h1l[...], gpos, NT)) + h * diag
        first_v[:, cols] = h * jnp.sqrt(num_ / den_)
        return carry

    k2 = []
    k1[0].wait_recv()
    gs1[0] = gp[c, 0] + rcgp[0]
    for d in (1, 3, 2):
        k2.append(send(gs1.at[0, (x + d) % 4], r1a.at[d - 1], rs_send.at[d], rs_recv.at[d], xdev(d)))
    k1[1].wait_recv()
    gs1[1] = gp[c, 1] + rcgp[1]
    for d in (1, 3, 2):
        k2.append(send(gs1.at[1, :, (z + d) % 4], r1b.at[d - 1], rs_send.at[3 + d], rs_recv.at[3 + d], zdev(d)))
    wait_all(gg2)
    gg3 = [
        send(gb.at[c], gb.at[c], gg_send.at[12], gg_recv.at[12], core),
        send(dg.at[c], dg.at[c], dg_send.at[6], dg_recv.at[6], core),
    ]
    late = pending[-8:]
    del pending[-8:]
    settle()
    pending.extend(late)
    fn[:, :512] = fp[:, :512]
    fn[:, 512:] = dot(fp[:, 512:], perm[...]).astype(BF16)
    wait_all(k2)
    ab2[0] = (gs1[0, x] + r1a[0]) + (r1a[1] + r1a[2])
    ab2[1] = (gs1[1, :, z] + r1b[0]) + (r1b[1] + r1b[2])
    k3 = []
    for d in (1, 3, 2):
        k3.append(send(ab2.at[0, (z + d) % 4], r2a.at[d - 1], rs_send.at[6 + d], rs_recv.at[6 + d], zdev(d)))
        k3.append(send(ab2.at[1, (x + d) % 4], r2b.at[d - 1], rs_send.at[9 + d], rs_recv.at[9 + d], xdev(d)))
    wait_all(gg3)
    lax.fori_loop(0, 2, first_body, 0)
    wait_all(k3)
    ab3[0] = (ab2[0, z] + r2a[0]) + (r2a[1] + r2a[2])
    ab3[1] = (ab2[1, x] + r2b[0]) + (r2b[1] + r2b[2])
    k4 = []
    for d in (1, 3, 2):
        k4.append(send(ab3, r3.at[d - 1], rs_send.at[12 + d], rs_recv.at[12 + d], ydev(d)))
    lax.fori_loop(2, 3, first_body, 0)
    settle()
    wait_all(k4)
    fin[...] = (ab3[...] + r3[0]) + (r3[1] + r3[2])

    sq = fin[0] * fin[0] + fin[1] * fin[1]
    nrm[...] = (sq[0:8] + sq[8:16]) + (sq[16:24] + sq[24:32])
    n1 = []
    for k in range(31):
        dc, dx, dz = (k + 1) // 16, (k + 1) // 4 % 4, (k + 1) % 4
        who = dev(yl, (c + dc) % 2, yh, (x + dx) % 4, (z + dz) % 4)
        n1.append(send(nrm, nrr.at[k], no_send.at[k], no_recv.at[k], who))
    dirh[c] = fin[yh]
    k5 = send(dirh.at[c], dirh.at[c], rs_send.at[16], rs_recv.at[16], core)
    lax.fori_loop(3, 4, first_body, 0)
    first_copy = pltpu.make_async_copy(first_v, first_hbm, local_sem.at[7])
    first_copy.start()
    wait_all(n1)
    settle()
    k5.wait_recv()
    tiles = nrm[...] + jnp.sum(nrr[...], axis=0)
    total = jnp.sum(jnp.sum(tiles, axis=1, keepdims=True), axis=0, keepdims=True)
    scale = jnp.sqrt(total / (1024 * width) + 1e-06)
    dirf[:, :128] = dirh[0] / scale
    dirf[:, 128:] = dirh[1] / scale
    dir_copy = pltpu.make_async_copy(dirf, dir_hbm, local_sem.at[6])
    dir_copy.start()
    second_copy.wait()
    first_copy.wait()
    dir_copy.wait()


def hand_out(a, b, c, a_out, b_out, c_out, av, bv, cv, sem):
    loads = [pltpu.make_async_copy(src, held, sem.at[k]) for k, (src, held) in enumerate(((a, av), (b, bv), (c, cv)))]
    stores = [
        pltpu.make_async_copy(held, dst, sem.at[3 + k])
        for k, (held, dst) in enumerate(((av, a_out), (bv, b_out), (cv, c_out)))
    ]
    for cp in loads:
        cp.start()
    for load, store in zip(loads, stores):
        load.wait()
        store.start()
    for cp in stores:
        cp.wait()


def shards(activations, dictionary, second_factor, first_codes, second_codes):
    tokens, rows = activations.shape
    sub, k1 = first_codes.shape[2:]
    k2 = second_codes.shape[3]
    v, dma = pltpu.VMEM, pltpu.SemaphoreType.DMA
    scratch = [
        v((2, 2, sub, rows), BF16), v((32, 32, rows), BF16), v((k1, k2), BF16), v((sub, k1), F32), v((sub, k2), F32),
        v((4, 2, 2, sub, 256), F32), v((4, 2, 32, 256), F32),
        v((4, 2, sub, 256), F32), v((4, 3, 32, 256), F32),
        v((4, sub, 256), F32), v((3, 32, 256), F32), v((4, sub, 256), F32),
        v((sub, k1), BF16), v((32, k1), F32), v((k1, k2), BF16), v((k2, k1), BF16),
        v((512, 512), BF16), v((128, 128), BF16), v((sub, k1), BF16), v((sub, k1), BF16),
        v((sub, k1), BF16), v((k1, sub), BF16),
        v((2, 4, 4, 32, k2), F32), v((2, 4, 4, 32, k1), BF16), v((2, 4, 4, 32, 128), F32),
        v((sub, k1), F32), v((sub, k2), F32), v((sub, k2), F32),
        v((2, 2, 4, 4, 32, 128), F32), v((2, 4, 4, 32, 128), F32), v((2, 4, 4, 32, 128), F32),
        v((3, 4, 32, 128), F32), v((3, 4, 32, 128), F32), v((2, 4, 32, 128), F32),
        v((3, 32, 128), F32), v((3, 32, 128), F32), v((2, 32, 128), F32), v((3, 2, 32, 128), F32),
        v((2, 32, 128), F32), v((2, 32, 128), F32), v((32, 256), F32),
        v((8, 128), F32), v((31, 8, 128), F32),
        dma((8,)), dma((3, 30)), dma((3, 30)), dma((4, 5)), dma((4, 5)), dma((38,)), dma((38,)), dma((13,)), dma((13,)),
        dma((7,)), dma((7,)), dma((18,)), dma((18,)), dma((31,)), dma((31,)),
    ]
    hbm = pl.BlockSpec(memory_space=pl.ANY)
    first, second, direction = pl.pallas_call(
        kernel,
        out_shape=(
            jax.ShapeDtypeStruct((sub, k1), F32),
            jax.ShapeDtypeStruct((sub, k2), F32),
            jax.ShapeDtypeStruct((32, k2), F32),
        ),
        in_specs=[hbm] * 5,
        out_specs=(hbm,) * 3,
        scratch_shapes=scratch,
        compiler_params=pltpu.CompilerParams(
            collective_id=0, has_side_effects=True, vmem_limit_bytes=60 * 1024 * 1024
        ),
        name="sweep",
    )(activations.reshape(2, 2, sub, rows), dictionary.T, second_factor, first_codes.reshape(sub, k1), second_codes.reshape(sub, k2))
    first, second, direction = pl.pallas_call(
        hand_out,
        out_shape=tuple(jax.ShapeDtypeStruct(o.shape, F32) for o in (first, second, direction)),
        in_specs=[hbm] * 3,
        out_specs=(hbm,) * 3,
        scratch_shapes=[v((sub, k1), F32), v((sub, k2), F32), v((32, k2), F32), dma((6,))],
        name="hand_out",
    )(first, second, direction)
    return first.reshape(first_codes.shape), second.reshape(second_codes.shape), direction


def solution(mesh):
    in_specs = (
        P("tok", "hid"),
        P("hid", "tok"),
        P(),
        P("tok", "hid", None, None),
        P("tok", "hid", None, None),
    )
    out_specs = (P("tok", "hid", None, None), P("tok", "hid", None, None), P("tok", None))
    return jax.shard_map(shards, mesh=mesh, in_specs=in_specs, out_specs=out_specs, check_vma=False)
```

```python
import functools

import jax
import jax.numpy as jnp
from jax import lax
from jax.experimental import pallas as pl
from jax.experimental.pallas import tpu as pltpu
from jax.sharding import PartitionSpec as P

F32 = jnp.float32
BF16 = jnp.bfloat16
MESH = pl.DeviceIdType.MESH
NN = (((1,), (0,)), ((), ()))
NT = (((1,), (1,)), ((), ()))


def dot(a, b, dims=NN):
    return lax.dot_general(a, b, dims, preferred_element_type=F32)


def split(a):
    hi = a.astype(BF16)
    return hi, (a - hi.astype(F32)).astype(BF16)


def dot3(a, b, dims=NN):
    ah, al = a
    bh, bl = b
    return dot(ah, bh, dims) + (dot(al, bh, dims) + dot(ah, bl, dims))


def pos_neg(g):
    p = split(jnp.maximum(g, 0.0))
    n = split(jnp.maximum(-g, 0.0))
    return p, n


ORDER = (
    (2, 0), (0, 2, 0, 1, 1), (0, 1, 1, 1), (0, 2, 0, 0, 0), (0, 1, 1, 0), (0, 2, 0, 1, 0), (0, 1, 0, 0),
    (0, 2, 0, 0, 1), (0, 1, 0, 1), (2, 1), (4, 0), (4, 1), (1, 1, 1, 0), (1, 2, 0, 0, 0), (0, 1, 2, 1), (1, 1, 0, 0),
    (1, 1, 0, 1), (0, 2, 0, 2, 1), (1, 2, 0, 0, 1), (1, 2, 0, 1, 0), (0, 1, 2, 0), (1, 1, 1, 1), (1, 2, 0, 1, 1),
    (0, 2, 0, 2, 0), (0, 2, 1, 0, 0), (0, 2, 2, 1, 1), (1, 1, 2, 0), (1, 2, 0, 2, 0), (1, 2, 1, 1, 0),
    (1, 2, 1, 0, 0), (1, 2, 2, 0, 0), (0, 2, 2, 0, 0), (1, 2, 1, 1, 1), (0, 2, 1, 1, 1), (1, 2, 0, 2, 1),
    (1, 1, 2, 1), (0, 2, 1, 1, 0), (1, 2, 2, 1, 1), (0, 2, 1, 2, 0), (1, 2, 1, 0, 1), (0, 2, 1, 2, 1),
    (0, 2, 2, 1, 0), (1, 2, 1, 2, 0), (1, 2, 3, 0, 0), (0, 2, 3, 1, 1), (0, 2, 1, 0, 1), (4, 2), (1, 2, 1, 2, 1),
    (0, 2, 3, 0, 0), (3, 0, 0), (1, 2, 2, 1, 0), (3, 0, 1), (0, 2, 2, 0, 1), (1, 2, 2, 0, 1), (0, 2, 2, 2, 1),
    (1, 2, 3, 1, 1), (1, 2, 2, 2, 1), (0, 2, 2, 2, 0), (3, 0, 2), (3, 0, 3), (1, 2, 2, 2, 0), (0, 2, 3, 1, 0),
    (3, 1, 0), (0, 2, 3, 0, 1), (1, 2, 3, 0, 1), (1, 2, 3, 1, 0), (3, 1, 1), (3, 1, 2), (0, 2, 3, 2, 1),
    (1, 2, 3, 2, 0), (1, 2, 3, 2, 1), (0, 2, 3, 2, 0), (3, 1, 3), (3, 2, 0), (3, 2, 1), (3, 2, 2), (3, 0, 4), (3, 3, 0),
    (3, 2, 3), (3, 3, 1),
)


def kernel(
    act_hbm, dt_hbm, s_hbm, h1_hbm, h2_hbm,
    first_hbm, second_hbm, dir_hbm,
    act, w, s, h1, h2,
    pl_f, pl_g, rc_f, rc_g, ys_f, ys_g, ry_f,
    fp, gown, sp, st, perm, eye, h1h, h1l, fn, ft,
    gsb, gb, dg, first_v, second_v, proj,
    gp, rcgp, gs1, r1a, r1b, ab2, r2a, r2b, ab3, r3, fin, dirh, dirf,
    nrm, nrr,
    local_sem, ga_send, ga_recv, fe_send, fe_recv, gs_send, gs_recv, gg_send, gg_recv,
    dg_send, dg_recv, rs_send, rs_recv, no_send, no_recv,
):
    hid = lax.axis_index("hid")
    tok = lax.axis_index("tok")
    yl, c = hid // 2, hid % 2
    yh, x, z = tok // 16, (tok // 4) % 4, tok % 4
    y = yh * 2 + yl
    sub = h1.shape[0]
    width = h2.shape[1]

    def dev(yl_, c_, yh_, x_, z_):
        return (yl_ * 2 + c_, yh_ * 16 + x_ * 4 + z_)

    core = dev(yl, 1 - c, yh, x, z)
    ylp = dev(1 - yl, c, yh, x, z)
    ylc = dev(1 - yl, 1 - c, yh, x, z)
    yhp = dev(yl, c, 1 - yh, x, z)

    def plane(dx, dz):
        return dev(yl, c, yh, (x + dx) % 4, (z + dz) % 4)

    def xdev(d):
        return plane(d, 0)

    def zdev(d):
        return plane(0, d)

    def ydev(d):
        yy = (y + d) % 4
        return dev(yy % 2, c, yy // 2, x, z)

    own_b = yh * 16 + x * 4 + z
    dcopy = pltpu.make_async_copy(dt_hbm, w.at[own_b], local_sem.at[1])
    dcopy.start()
    scopy = pltpu.make_async_copy(s_hbm, s, local_sem.at[2])
    scopy.start()
    h1copy = pltpu.make_async_copy(h1_hbm, h1, local_sem.at[3])
    h1copy.start()
    h2copy = pltpu.make_async_copy(h2_hbm, h2, local_sem.at[4])
    h2copy.start()
    acopy = pltpu.make_async_copy(act_hbm, act, local_sem.at[0])
    acopy.start()

    barrier = pltpu.get_barrier_semaphore()
    peers = [xdev(1), xdev(3), zdev(1), zdev(3), ydev(1), ydev(2), ydev(3), core, ylc]
    for who in peers:
        pl.semaphore_signal(barrier, inc=1, device_id=who, device_id_type=MESH)
    pl.semaphore_wait(barrier, len(peers))

    pending = []

    def send(src, dst, ss, rs, who):
        cp = pltpu.make_async_remote_copy(
            src_ref=src, dst_ref=dst, send_sem=ss, recv_sem=rs, device_id=who, device_id_type=MESH
        )
        cp.start()
        pending.append(cp)
        return cp

    def settle():
        for cp in pending:
            cp.wait_send()
        pending.clear()

    def wait_all(cps):
        for cp in cps:
            cp.wait_recv()

    def part(o):
        p = (yh + o) % 2
        u = x + p * (z - x)
        v = z + p * (x - z)
        return p, u, v

    def blk(p, u_, v_):
        return p * 16 + u_ * (4 - 3 * p) + v_ * (1 + 3 * p)

    DU = (0, 3, 1, 2)

    def gdev(o, du, dv):
        p, u, v = part(o)
        u_, v_ = (u + du) % 4, (v + dv) % 4
        return (hid, yh * 16 + u_ * (4 - 3 * p) + v_ * (1 + 3 * p))

    def gblk(o, du, dv):
        p, u, v = part(o)
        return blk(p, (u + du) % 4, (v + dv) % 4)

    gd = {}
    arrived = set()

    def need(*key):
        if key not in arrived:
            arrived.add(key)
            gd[key].wait_recv()

    def gsend(key, k, b, who, r, hbm=False):
        o = key[0]
        dst = w.at[b, pl.ds(16 * r, 16)]
        src = dt_hbm.at[pl.ds(16 * r, 16)] if hbm else dst
        gd[key] = send(src, dst, ga_send.at[o, k], ga_recv.at[o, k], who)

    def own_here(o, r):
        if o == 1:
            need(2, r)

    def step(key):
        o = key[0]
        if o == 2:
            gsend(key, key[1], own_b, yhp, key[1], True)
        elif key[1] == 1:
            _, _, sg, r = key
            if sg < 2:
                own_here(o, r)
                gsend(key, sg * 2 + r, gblk(o, 0, 0), gdev(o, 3 if sg else 1, 0), r, o == 0)
            else:
                need(o, 1, r, r)
                gsend(key, 4 + r, gblk(o, 1 if r else 3, 0), gdev(o, 3 if r else 1, 0), r)
        else:
            _, _, i, sg, r = key
            k = 6 + 6 * i
            if sg < 2:
                if i == 0:
                    own_here(o, r)
                elif i < 3:
                    need(o, 1, i - 1, r)
                else:
                    need(o, 1, 2, r)
                gsend(key, k + sg * 2 + r, gblk(o, DU[i], 0), gdev(o, 0, 3 if sg else 1), r, o == 0 and i == 0)
            else:
                need(o, 2, i, r, r)
                gsend(key, k + 4 + r, gblk(o, DU[i], 1 if r else 3), gdev(o, 0, 3 if r else 1), r)

    def need_group(i):
        for o in (0, 1):
            for r in (0, 1):
                own_here(o, r)
                if i in (1, 2):
                    need(o, 1, i - 1, r)
                if i == 3:
                    need(o, 1, 2, r)
                for sg in (0, 1, 2):
                    need(o, 2, i, sg, r)

    fd = {}

    def chunk_of(o, i):
        p, u, v = part(o)
        return p * 4 + (u + DU[i]) % 4

    def weights(i):
        rows = []
        for o in (0, 1):
            p, u, v = part(o)
            rows += [w[blk(p, (u + DU[i]) % 4, j)] for j in range(4)]
        return jnp.concatenate(rows, axis=0)

    def group_g(i):
        need_group(i)
        lrows = jnp.concatenate([w[x * 4 + z], w[16 + x * 4 + z]], axis=0)
        g = dot(lrows, weights(i), NT)
        pl_g[i] = g.reshape(2, 32, g.shape[1])
        fd[i, 0] = send(pl_g.at[i, 1 - c], rc_g.at[i, 0], fe_send.at[i, 0], fe_recv.at[i, 0], core)
        if i < 3:
            return
        fd[i, 1] = send(pl_g.at[i, c], rc_g.at[i, 1], fe_send.at[i, 1], fe_recv.at[i, 1], ylp)
        fd[i, 2] = send(pl_g.at[i, 1 - c], rc_g.at[i, 2], fe_send.at[i, 2], fe_recv.at[i, 2], ylc)

    def group_f(i, other):
        cc = 1 - c if other else c
        a = act[:, cc].reshape(2 * sub, act.shape[3])
        pl_f[i, cc] = dot(a, weights(i), NT).reshape(2, sub, 256)
        if other:
            fd[i, 3] = send(pl_f.at[i, cc], rc_f.at[i], fe_send.at[i, 3], fe_recv.at[i, 3], core)

    def reduce_core(i):
        if i < 3:
            fd[i, 0].wait_recv()
            ys_g[i] = pl_g[i, c] + rc_g[i, 0]
            fd[i, 1] = send(ys_g.at[i], rc_g.at[i, 1], fe_send.at[i, 1], fe_recv.at[i, 1], ylp)
        fd[i, 3].wait_recv()
        out, back = (ys_f.at[i], ry_f.at[i])
        out[...] = (pl_f[i, c, 1 - yl] + rc_f[i, 1 - yl]).astype(out.dtype)
        fd[i, 4] = send(out, back, fe_send.at[i, 4], fe_recv.at[i, 4], ylp)

    def lanes(q):
        return pl.ds(pl.multiple_of(q * 128, 128), 128)

    def reduce_g(i):
        if i < 3:
            fd[i, 1].wait_recv()
            g = ys_g[i] + rc_g[i, 1]
        else:
            for k in range(3):
                fd[i, k].wait_recv()
            g = (pl_g[i, c] + rc_g[i, 0]) + (rc_g[i, 1] + rc_g[i, 2])
        gown[:, lanes(chunk_of(0, i))] = g[:, :128]
        gown[:, lanes(chunk_of(1, i))] = g[:, 128:]

    def reduce_f(i):
        fd[i, 4].wait_recv()
        back = ry_f[i]
        f = ((pl_f[i, c, yl] + rc_f[i, yl]) + back).astype(BF16)
        total = None
        for o in (0, 1):
            p, u, v = part(o)
            ui = (u + DU[i]) % 4
            q = p * 4 + ui
            fo = f[:, 128 * o:128 * o + 128]
            fp[:, lanes(q)] = fo
            term = dot(fo, sp[lanes(q), :])
            total = term if total is None else total + term
            turned = dot(eye[...], fo, NT).astype(BF16)
            for j in range(4):
                at = p * 512 + ui * (128 - 96 * p) + j * (32 + 96 * p)
                ft[pl.ds(pl.multiple_of(at, 32), 32), :] = turned[j * 32:j * 32 + 32]
        proj[...] = total if i == 0 else proj[...] + total

    def prepare_a():
        n_i = lax.broadcasted_iota(jnp.int32, (512, 512), 0)
        r_i = lax.broadcasted_iota(jnp.int32, (512, 512), 1)
        swapped = ((n_i // 32) % 4) * 128 + (n_i // 128) * 32 + n_i % 32
        perm[...] = (r_i == swapped).astype(F32).astype(BF16)
        eye[...] = (r_i == n_i)[:128, :128].astype(F32).astype(BF16)

    def prepare_b():
        scopy.wait()
        sp[0:512] = s[0:512]
        for a in range(4):
            for b in range(4):
                to, at = 512 + a * 128 + b * 32, 512 + b * 128 + a * 32
                sp[to:to + 32] = s[at:at + 32]
        st[...] = s[...].astype(F32).T.astype(BF16)

    def prepare_c():
        h1copy.wait()
        hh, hl = split(h1[...])
        h1h[:, :512] = hh[:, :512]
        h1l[:, :512] = hl[:, :512]
        h1h[:, 512:] = dot(hh[:, 512:], perm[...]).astype(BF16)
        h1l[:, 512:] = dot(hl[:, 512:], perm[...]).astype(BF16)

    for op in ORDER:
        if op[0] < 3:
            step(op)
        elif op[0] == 3:
            _, i, k = op
            if k == 0:
                if i == 0:
                    dcopy.wait()
                    acopy.wait()
                group_g(i)
            elif k < 3:
                group_f(i, k == 1)
            elif k == 4:
                reduce_f(i)
            else:
                reduce_core(i)
                if i > 0:
                    reduce_g(i - 1)
        else:
            (prepare_a, prepare_b, prepare_c)[op[1]]()
    reduce_g(2)
    reduce_g(3)

    g = gown[...]
    gh, gl = split(g)
    gsb[c, x, z] = dot(gh, sp[...]) + dot(gl, sp[...])

    half = width // 2

    def gs_part(o, bx, bz):
        return gsb.at[c, bx, bz, :, pl.ds(half * o, half)]

    def gs_go(ref, k, who):
        return send(ref, ref, gs_send.at[k], gs_recv.at[k], who)

    g1 = {}
    for d in (1, 3, 2):
        g1[0, d] = gs_go(gs_part(0, x, z), d - 1, xdev(d))
        g1[1, d] = gs_go(gs_part(1, x, z), 2 + d, zdev(d))
    g2 = {}
    for d in (1, 3, 2):
        g2[0, 0, d] = gs_go(gs_part(0, x, z), 5 + d, zdev(d))
        g2[1, 0, d] = gs_go(gs_part(1, x, z), 17 + d, xdev(d))
    group_f(3, False)
    reduce_core(3)

    at_diag = c * 512 + (x + c * (z - x)) * 128 + (z + c * (x - z)) * 32
    lane = lax.broadcasted_iota(jnp.int32, g.shape, 1)
    row = lax.broadcasted_iota(jnp.int32, g.shape, 0)
    on = lane == at_diag + row
    reduce_f(1)
    gb[c, x, z] = jnp.where(on, 0.0, g).astype(BF16)
    dg[c, x, z] = jnp.broadcast_to(jnp.sum(jnp.where(on, g, 0.0), axis=1, keepdims=True), (32, 128))

    for j in (1, 3, 2):
        for o in (0, 1):
            g1[o, j].wait_recv()
            for d in (1, 3, 2):
                ref = gs_part(o, (x + 4 - j) % 4, z) if o == 0 else gs_part(o, x, (z + 4 - j) % 4)
                g2[o, j, d] = gs_go(ref, 5 + 12 * o + 3 * j + d, zdev(d) if o == 0 else xdev(d))
    g3 = [
        gs_go(gsb.at[c, :, z, :, pl.ds(0, half)], 30, core),
        gs_go(gsb.at[c, x, :, :, pl.ds(half, half)], 34, core),
    ]
    gg1 = []
    for d in (1, 3, 2):
        a = gb.at[c, x, z, :, pl.ds(0, 512)]
        b = gb.at[c, x, z, :, pl.ds(512, 512)]
        e = dg.at[c, x, z]
        gg1.append(send(a, a, gg_send.at[d - 1], gg_recv.at[d - 1], xdev(d)))
        gg1.append(send(b, b, gg_send.at[3 + d - 1], gg_recv.at[3 + d - 1], zdev(d)))
        gg1.append(send(e, e, dg_send.at[d - 1], dg_recv.at[d - 1], xdev(d)))
    wait_all(gg1)
    gg2 = []
    for d in (1, 3, 2):
        a = gb.at[c, :, z, :, pl.ds(0, 512)]
        b = gb.at[c, x, :, :, pl.ds(512, 512)]
        e = dg.at[c, :, z]
        gg2.append(send(a, a, gg_send.at[6 + d - 1], gg_recv.at[6 + d - 1], zdev(d)))
        gg2.append(send(b, b, gg_send.at[9 + d - 1], gg_recv.at[9 + d - 1], xdev(d)))
        gg2.append(send(e, e, dg_send.at[3 + d - 1], dg_recv.at[3 + d - 1], zdev(d)))
    for d in (1, 3, 2):
        for o in (0, 1):
            for j in (0, 1, 3, 2):
                g2[o, j, d].wait_recv()
            if o == 0:
                ref = gsb.at[c, :, (z + 4 - d) % 4, :, pl.ds(0, half)]
            else:
                ref = gsb.at[c, (x + 4 - d) % 4, :, :, pl.ds(half, half)]
            g3.append(gs_go(ref, 30 + 4 * o + d, core))
    reduce_f(2)
    h2copy.wait()
    reduce_f(3)
    wait_all(g3)

    gs = gsb[...].reshape(1024, width)
    gsh, gsl = split(gs)
    inner = dot(st[...], gsh) + dot(st[...], gsl)
    ip, im = pos_neg(inner)
    h2v = h2[...]
    h2s = split(h2v)
    pr = proj[...]
    num = jnp.maximum(pr, 0.0) + dot3(h2s, im)
    den = jnp.maximum(-pr, 0.0) + dot3(h2s, ip)
    second = h2v * jnp.sqrt(num / den)
    second_v[...] = second
    second_copy = pltpu.make_async_copy(second_v, second_hbm, local_sem.at[5])
    second_copy.start()

    sn = split(second)
    k1 = []
    for p in (0, 1):
        rows = slice(512 * p, 512 * p + 512)
        res = dot3((gsh[rows], gsl[rows]), sn, NT) - ft[rows, :].astype(F32)
        gr = dot3(split(res), sn)
        gp[0, p] = gr[:, :128].reshape(4, 4, 32, 128)
        gp[1, p] = gr[:, 128:].reshape(4, 4, 32, 128)
        k1.append(send(gp.at[1 - c, p], rcgp.at[p], rs_send.at[17 * p], rs_recv.at[17 * p], core))

    def first_body(j, carry):
        gt = gb[j // 2, pl.ds((j % 2) * 2, 2)].reshape(256, 1024)
        diag = dg[j // 2, pl.ds((j % 2) * 2, 2)].reshape(256, 128).T[0:1]
        gpos, gneg = jnp.maximum(gt, 0), jnp.maximum(-gt, 0)
        cols = pl.ds(pl.multiple_of(j * 256, 256), 256)
        f = fn[:, cols].astype(F32)
        h = h1[:, cols]
        num_ = jnp.maximum(f, 0.0) + (dot(h1h[...], gneg, NT) + dot(h1l[...], gneg, NT))
        den_ = jnp.maximum(-f, 0.0) + (dot(h1h[...], gpos, NT) + dot(h1l[...], gpos, NT)) + h * diag
        first_v[:, cols] = h * jnp.sqrt(num_ / den_)
        return carry

    k2 = []
    k1[0].wait_recv()
    gs1[0] = gp[c, 0] + rcgp[0]
    for d in (1, 3, 2):
        k2.append(send(gs1.at[0, (x + d) % 4], r1a.at[d - 1], rs_send.at[d], rs_recv.at[d], xdev(d)))
    k1[1].wait_recv()
    gs1[1] = gp[c, 1] + rcgp[1]
    for d in (1, 3, 2):
        k2.append(send(gs1.at[1, :, (z + d) % 4], r1b.at[d - 1], rs_send.at[3 + d], rs_recv.at[3 + d], zdev(d)))
    wait_all(gg2)
    gg3 = [
        send(gb.at[c], gb.at[c], gg_send.at[12], gg_recv.at[12], core),
        send(dg.at[c], dg.at[c], dg_send.at[6], dg_recv.at[6], core),
    ]
    late = pending[-8:]
    del pending[-8:]
    settle()
    pending.extend(late)
    fn[:, :512] = fp[:, :512]
    fn[:, 512:] = dot(fp[:, 512:], perm[...]).astype(BF16)
    wait_all(k2)
    ab2[0] = (gs1[0, x] + r1a[0]) + (r1a[1] + r1a[2])
    ab2[1] = (gs1[1, :, z] + r1b[0]) + (r1b[1] + r1b[2])
    k3 = []
    for d in (1, 3, 2):
        k3.append(send(ab2.at[0, (z + d) % 4], r2a.at[d - 1], rs_send.at[6 + d], rs_recv.at[6 + d], zdev(d)))
        k3.append(send(ab2.at[1, (x + d) % 4], r2b.at[d - 1], rs_send.at[9 + d], rs_recv.at[9 + d], xdev(d)))
    wait_all(gg3)
    lax.fori_loop(0, 2, first_body, 0)
    wait_all(k3)
    ab3[0] = (ab2[0, z] + r2a[0]) + (r2a[1] + r2a[2])
    ab3[1] = (ab2[1, x] + r2b[0]) + (r2b[1] + r2b[2])
    k4 = []
    for d in (1, 3, 2):
        k4.append(send(ab3, r3.at[d - 1], rs_send.at[12 + d], rs_recv.at[12 + d], ydev(d)))
    lax.fori_loop(2, 3, first_body, 0)
    settle()
    wait_all(k4)
    fin[...] = (ab3[...] + r3[0]) + (r3[1] + r3[2])

    sq = fin[0] * fin[0] + fin[1] * fin[1]
    nrm[...] = (sq[0:8] + sq[8:16]) + (sq[16:24] + sq[24:32])
    n1 = []
    for k in range(31):
        dc, dx, dz = (k + 1) // 16, (k + 1) // 4 % 4, (k + 1) % 4
        who = dev(yl, (c + dc) % 2, yh, (x + dx) % 4, (z + dz) % 4)
        n1.append(send(nrm, nrr.at[k], no_send.at[k], no_recv.at[k], who))
    dirh[c] = fin[yh]
    k5 = send(dirh.at[c], dirh.at[c], rs_send.at[16], rs_recv.at[16], core)
    lax.fori_loop(3, 4, first_body, 0)
    first_copy = pltpu.make_async_copy(first_v, first_hbm, local_sem.at[7])
    first_copy.start()
    wait_all(n1)
    k5.wait_recv()
    tiles = nrm[...] + jnp.sum(nrr[...], axis=0)
    total = jnp.sum(jnp.sum(tiles, axis=1, keepdims=True), axis=0, keepdims=True)
    scale = jnp.sqrt(total / (1024 * width) + 1e-06)
    dirf[:, :128] = dirh[0] / scale
    dirf[:, 128:] = dirh[1] / scale
    dir_copy = pltpu.make_async_copy(dirf, dir_hbm, local_sem.at[6])
    dir_copy.start()
    settle()
    second_copy.wait()
    first_copy.wait()
    dir_copy.wait()


def hand_out(a, b, c, a_out, b_out, c_out, av, bv, cv, sem):
    loads = [pltpu.make_async_copy(src, held, sem.at[k]) for k, (src, held) in enumerate(((a, av), (b, bv), (c, cv)))]
    stores = [
        pltpu.make_async_copy(held, dst, sem.at[3 + k])
        for k, (held, dst) in enumerate(((av, a_out), (bv, b_out), (cv, c_out)))
    ]
    for cp in loads:
        cp.start()
    for load, store in zip(loads, stores):
        load.wait()
        store.start()
    for cp in stores:
        cp.wait()


def shards(activations, dictionary, second_factor, first_codes, second_codes):
    tokens, rows = activations.shape
    sub, k1 = first_codes.shape[2:]
    k2 = second_codes.shape[3]
    v, dma = pltpu.VMEM, pltpu.SemaphoreType.DMA
    scratch = [
        v((2, 2, sub, rows), BF16), v((32, 32, rows), BF16), v((k1, k2), BF16), v((sub, k1), F32), v((sub, k2), F32),
        v((4, 2, 2, sub, 256), F32), v((4, 2, 32, 256), F32),
        v((4, 2, sub, 256), F32), v((4, 3, 32, 256), F32),
        v((4, sub, 256), F32), v((3, 32, 256), F32), v((4, sub, 256), F32),
        v((sub, k1), BF16), v((32, k1), F32), v((k1, k2), BF16), v((k2, k1), BF16),
        v((512, 512), BF16), v((128, 128), BF16), v((sub, k1), BF16), v((sub, k1), BF16),
        v((sub, k1), BF16), v((k1, sub), BF16),
        v((2, 4, 4, 32, k2), F32), v((2, 4, 4, 32, k1), BF16), v((2, 4, 4, 32, 128), F32),
        v((sub, k1), F32), v((sub, k2), F32), v((sub, k2), F32),
        v((2, 2, 4, 4, 32, 128), F32), v((2, 4, 4, 32, 128), F32), v((2, 4, 4, 32, 128), F32),
        v((3, 4, 32, 128), F32), v((3, 4, 32, 128), F32), v((2, 4, 32, 128), F32),
        v((3, 32, 128), F32), v((3, 32, 128), F32), v((2, 32, 128), F32), v((3, 2, 32, 128), F32),
        v((2, 32, 128), F32), v((2, 32, 128), F32), v((32, 256), F32),
        v((8, 128), F32), v((31, 8, 128), F32),
        dma((8,)), dma((3, 30)), dma((3, 30)), dma((4, 5)), dma((4, 5)), dma((38,)), dma((38,)), dma((13,)), dma((13,)),
        dma((7,)), dma((7,)), dma((18,)), dma((18,)), dma((31,)), dma((31,)),
    ]
    hbm = pl.BlockSpec(memory_space=pl.ANY)
    first, second, direction = pl.pallas_call(
        kernel,
        out_shape=(
            jax.ShapeDtypeStruct((sub, k1), F32),
            jax.ShapeDtypeStruct((sub, k2), F32),
            jax.ShapeDtypeStruct((32, k2), F32),
        ),
        in_specs=[hbm] * 5,
        out_specs=(hbm,) * 3,
        scratch_shapes=scratch,
        compiler_params=pltpu.CompilerParams(
            collective_id=0, has_side_effects=True, vmem_limit_bytes=60 * 1024 * 1024
        ),
        name="sweep",
    )(activations.reshape(2, 2, sub, rows), dictionary.T, second_factor, first_codes.reshape(sub, k1), second_codes.reshape(sub, k2))
    first, second, direction = pl.pallas_call(
        hand_out,
        out_shape=tuple(jax.ShapeDtypeStruct(o.shape, F32) for o in (first, second, direction)),
        in_specs=[hbm] * 3,
        out_specs=(hbm,) * 3,
        scratch_shapes=[v((sub, k1), F32), v((sub, k2), F32), v((32, k2), F32), dma((6,))],
        name="hand_out",
    )(first, second, direction)
    return first.reshape(first_codes.shape), second.reshape(second_codes.shape), direction


def solution(mesh):
    in_specs = (
        P("tok", "hid"),
        P("hid", "tok"),
        P(),
        P("tok", "hid", None, None),
        P("tok", "hid", None, None),
    )
    out_specs = (P("tok", "hid", None, None), P("tok", "hid", None, None), P("tok", None))
    return jax.shard_map(shards, mesh=mesh, in_specs=in_specs, out_specs=out_specs, check_vma=False)
```
